512 devices in a mesh: dp: 64 (over x_lo, z, core), tensor: 8 (over y, x_hi).
Axes of the slice: x: 4 (x_hi: 2, x_lo: 2; x = x_hi * 2 + x_lo), y: 4, z: 16, core: 2. Of those that a mesh axis runs over, the one named last changes fastest.
Arguments:
- patches: bfloat16 [14336, 6144], P('dp'), as said below
- qkv_weight: bfloat16 [6144, 3, 3072], P('dp', None, 'tensor'), as said below
- out_grad: bfloat16 [14336, 3072], P('dp', 'tensor'), may hold values from -6 to 6
- image_starts: int32 [64, 224], replicated, may hold values from -1 to 14320, as said below
Outputs:
- attended: bfloat16 [14336, 3072], P('dp', 'tensor')
- patch_grad: bfloat16 [14336, 6144], P('dp', 'tensor')
The draws below stay inside these ranges and needn't reach their ends.
Inputs may be any that keep to these rules, and one draw needn't show every extreme that they name: `patches`: patches entries lie within -8 to 8. `qkv_weight`: entries lie within 170 / sqrt(6144) in magnitude. `image_starts`: entry (s, r) is the row of the whole packed array at which the image holding row r of shard s begins, or -1 for an empty row. On every shard the images fill rows 0 to some count without gaps, each spanning a multiple of 16 rows, and empty rows follow. For s below 64 / 2, shards s and s + 64 / 2 hold 320 image rows together; one of them holds more than 160 rows and has an image beginning at its row 160. Some shard holds 224 rows.
All inputs are finite; a program needn't handle non-finite values.
Results may differ from the reference program's by a relative error of at most 0.02.
The reference program's roundings to bfloat16 on the way count: a program that leaves them out, or rounds other values in their place, can miss the bound.
Values may be sent and summed in bfloat16 or wider, within the bound.
A program may use at most 128 MiB of HBM per device.

```python
import jax
import jax.numpy as jnp
from jax import lax

D = 6144
HEADS = 24
HD = 128
UNIT = 16
CAP = 160
MOVE = 64
SLOT = 224
TOKENS = 14336
N_DP = 64
N_TENSOR = 8


def draw_patches(key, part):
    key = jax.random.fold_in(key, 11)
    normal_draw = jnp.clip(jax.random.normal(key, (TOKENS, D), jnp.float32), -6.0, 6.0)
    return normal_draw.astype(jnp.bfloat16)


def draw_qkv_weight(key, part):
    key = jax.random.fold_in(key, 23)
    weight = jnp.clip(jax.random.normal(key, (D, 3, HEADS * HD), jnp.float32), -6.0, 6.0) * D ** (-0.5)
    return weight.astype(jnp.bfloat16)


def draw_image_starts(key, part):
    key = jax.random.fold_in(key, 37)
    pair_count = N_DP // 2
    cap_units = CAP // UNIT
    move_units = MOVE // UNIT
    slot_units = cap_units + move_units
    moved_units = jax.random.randint(jax.random.fold_in(key, 1), (pair_count,), move_units // 2, move_units + 1)
    full_pair = jax.random.randint(jax.random.fold_in(key, 2), (), 0, pair_count)
    moved_units = jnp.where(jnp.arange(pair_count) == full_pair, move_units, moved_units)
    heavy_side = jax.random.randint(jax.random.fold_in(key, 3), (pair_count,), 0, 2)
    overfull = jnp.concatenate([heavy_side == 0, heavy_side == 1])
    moved_all = jnp.concatenate([moved_units, moved_units])
    used_units = jnp.where(overfull, cap_units + moved_all, cap_units - moved_all)
    unit_index = jnp.arange(slot_units)
    coin_flip = jax.random.randint(jax.random.fold_in(key, 4), (N_DP, slot_units), 0, 3) == 0
    starts_here = coin_flip | (unit_index == 0)[None, :] | overfull[:, None] & (unit_index == cap_units)[None, :]
    start_mark = jnp.where(starts_here, unit_index[None, :], 0)
    image_first = lax.cummax(start_mark, axis=1)
    row_start = jnp.arange(N_DP)[:, None] * SLOT + image_first * UNIT
    live_units = unit_index[None, :] < used_units[:, None]
    image_ids = jnp.where(live_units, row_start, -1)
    return jnp.repeat(image_ids, UNIT, axis=1).astype(jnp.int32)


def block_scale(key, dims, cuts, least, top_value):
    def one(axis_at, blocks):
        heights = jax.random.uniform(jax.random.fold_in(jax.random.fold_in(key, 6), axis_at), (blocks,), jnp.float32, least / len(cuts), top_value / len(cuts))
        return jnp.repeat(jnp.exp(heights), dims[axis_at] // blocks).reshape((-1,) + (1,) * (len(dims) - axis_at - 1))

    level = one(*cuts[0])
    for cut in cuts[1:]:
        level = level * one(*cut)
    return level


def centred(key, dims, width, reach, cuts=(), kind=jnp.bfloat16):
    values = jax.random.normal(key, dims, jnp.float32) * width
    if len(cuts) > 0:
        values = block_scale(key, dims, cuts, -0.22, 0.18) * values
    return jnp.clip(values, min=-reach, max=reach).astype(kind)


def setup_inputs(seed: int = 0) -> dict:
    arg_keys = jax.random.split(jax.random.key(seed), 5)
    return {
        "patches": draw_patches(jax.random.fold_in(arg_keys[4], 71), 0),
        "qkv_weight": draw_qkv_weight(jax.random.fold_in(arg_keys[4], 71), 0),
        "out_grad": centred(arg_keys[2], (TOKENS, HEADS * HD), 1.0, 6.0, ((0, 64), (1, 8))),
        "image_starts": draw_image_starts(jax.random.fold_in(arg_keys[4], 71), 0),
    }


def attend(qkv_rows, image_ids, out_grad):
    score_scale = HD ** -0.5
    row_count = qkv_rows.shape[0]
    head_count = qkv_rows.shape[2]
    query_rows = qkv_rows[:, 0].astype(jnp.float32)
    key_rows = qkv_rows[:, 1].astype(jnp.float32)
    value_rows = qkv_rows[:, 2].astype(jnp.float32)
    scores = jnp.einsum('qhd,khd->hqk', query_rows, key_rows) * score_scale
    allowed = (image_ids[:, None] == image_ids[None, :]) & (image_ids[None, :] >= 0)
    live_rows = (image_ids >= 0).astype(jnp.float32)
    logits = jnp.where(allowed[None], scores, -1e30)
    top_score = jnp.max(logits, axis=-1, keepdims=True)
    expo = jnp.exp(logits - top_score)
    attn_probs = expo / jnp.sum(expo, axis=-1, keepdims=True) * live_rows[None, :, None]
    probs_low = attn_probs.astype(jnp.bfloat16).astype(jnp.float32)
    attended = jnp.einsum('hqk,khd->qhd', probs_low, value_rows).astype(jnp.bfloat16)
    grad_out = out_grad.reshape(row_count, head_count, HD).astype(jnp.float32)
    grad_probs = jnp.einsum('qhd,khd->hqk', grad_out, value_rows)
    grad_value = jnp.einsum('hqk,qhd->khd', probs_low, grad_out).astype(jnp.bfloat16)
    row_delta = jnp.sum(attn_probs * grad_probs, axis=-1, keepdims=True)
    grad_scores = (attn_probs * (grad_probs - row_delta) * score_scale).astype(jnp.bfloat16).astype(jnp.float32)
    grad_query = jnp.einsum('hqk,khd->qhd', grad_scores, key_rows).astype(jnp.bfloat16)
    grad_key = jnp.einsum('hqk,qhd->khd', grad_scores, query_rows).astype(jnp.bfloat16)
    grad_qkv = jnp.stack([grad_query, grad_key, grad_value], axis=1)
    return attended.reshape(row_count, head_count * HD), grad_qkv.reshape(row_count, 3, head_count * HD)


def reference(patches, qkv_weight, out_grad, image_starts):
    flat_weight = qkv_weight.reshape(D, 3 * HEADS * HD)
    group_width = HEADS * HD // N_TENSOR

    def shard_pass(inputs):
        rows, image_ids, grads = inputs
        qkv_rows = jnp.dot(rows, flat_weight, preferred_element_type=jnp.float32).astype(jnp.bfloat16)
        attended, grad_qkv = attend(qkv_rows.reshape(SLOT, 3, HEADS, HD), image_ids, grads)
        total = jnp.zeros((SLOT, D), jnp.float32)
        for group in range(N_TENSOR):
            lower = group * group_width
            grad_piece = grad_qkv[:, :, lower:lower + group_width].reshape(SLOT, 3 * group_width)
            weight_piece = qkv_weight[:, :, lower:lower + group_width].reshape(D, 3 * group_width)
            term = lax.dot_general(grad_piece, weight_piece, (((1,), (1,)), ((), ())), preferred_element_type=jnp.float32)
            term = lax.optimization_barrier(term.astype(jnp.bfloat16))
            total = total + term.astype(jnp.float32)
        return attended, total.astype(jnp.bfloat16)

    attended, patch_grad = lax.map(shard_pass, (patches.reshape(N_DP, SLOT, D), image_starts, out_grad.reshape(N_DP, SLOT, HEADS * HD)))
    return attended.reshape(TOKENS, HEADS * HD), patch_grad.reshape(TOKENS, D)
```

```python
import functools

import jax
import jax.numpy as jnp
from jax import lax
from jax.experimental import pallas as pl
from jax.experimental.pallas import tpu as pltpu
from jax.sharding import PartitionSpec as P

HD = 128
NZ = 16
NY = 4
MESH = pl.DeviceIdType.MESH
PIECE = 384


def attend_head(query, key, value, grad_out, allowed, live):
    score_scale = HD ** (-0.5)
    nt = (((1,), (1,)), ((), ()))
    tn = (((0,), (0,)), ((), ()))
    scores = lax.dot_general(query, key, nt, preferred_element_type=jnp.float32) * score_scale
    logits = jnp.where(allowed, scores, -1e30)
    top_score = jnp.max(logits, axis=-1, keepdims=True)
    expo = jnp.exp(logits - top_score)
    probs = expo / jnp.sum(expo, axis=-1, keepdims=True) * live
    low = probs.astype(jnp.bfloat16)
    attended = jnp.dot(low, value, preferred_element_type=jnp.float32).astype(jnp.bfloat16)
    grad_probs = lax.dot_general(grad_out, value, nt, preferred_element_type=jnp.float32)
    grad_value = lax.dot_general(low, grad_out, tn, preferred_element_type=jnp.float32).astype(jnp.bfloat16)
    row_delta = jnp.sum(probs * grad_probs, axis=-1, keepdims=True)
    grad_scores = (probs * (grad_probs - row_delta) * score_scale).astype(jnp.bfloat16)
    grad_query = jnp.dot(grad_scores, key, preferred_element_type=jnp.float32).astype(jnp.bfloat16)
    grad_key = lax.dot_general(grad_scores, query, tn, preferred_element_type=jnp.float32).astype(jnp.bfloat16)
    return attended, grad_query, grad_key, grad_value


def kernel(
    x_ref, w_ref, g_ref, idc_ref, idr_ref, att_ref, out_ref,
    wbuf, acc, qkv, gbuf, sbuf, rbuf, zs, zr, xs, xr, cs, cr, ts, tr,
):
    dp, t = lax.axis_index("dp"), lax.axis_index("tensor")
    xl, z, c = dp // (2 * NZ), (dp // 2) % NZ, dp % 2
    y, xh = t // 2, t % 2
    heads = w_ref.shape[1] // (3 * HD)
    width = heads * HD

    def dev(xl_, z_, c_):
        return (xl_ * (2 * NZ) + z_ * 2 + c_, t)

    z_next = (dev(xl, (z + 1) % NZ, c), dev(xl, (z + NZ - 1) % NZ, c))
    x_dev = dev(1 - xl, z, c)
    c_dev = dev(xl, z, 1 - c)
    peers = [(dp, ((y + j // 2) % NY) * 2 + (xh + j) % 2) for j in range(1, 8)]

    barrier = pltpu.get_barrier_semaphore()
    everyone = [*z_next, x_dev, c_dev, *peers]
    for other in everyone:
        pl.semaphore_signal(barrier, inc=1, device_id=other, device_id_type=MESH)
    pl.semaphore_wait(barrier, len(everyone))

    def origin(d, s):
        return (z - s + NZ) % NZ if d == 0 else (z + s) % NZ

    def part(xl_, z_, c_, p):
        return wbuf.at[xl_ * (2 * NZ) + z_ * 2 + c_, :, p * PIECE : (p + 1) * PIECE]

    def whole(xl_, z_, c_):
        return wbuf.at[xl_ * (2 * NZ) + z_ * 2 + c_]

    def z_ref(zo, p):
        return part(1 - xl, zo, c, 0) if p == 0 else part(xl, zo, c, p - 1)

    def remote(ref, send, recv, device):
        return pltpu.make_async_remote_copy(
            src_ref=ref, dst_ref=ref, send_sem=send, recv_sem=recv, device_id=device, device_id_type=MESH
        )

    def z_send(d, s, p):
        return remote(z_ref(origin(d, s - 1), p), zs.at[d, s, p], zr.at[d, s, p], z_next[d])

    def z_recv(d, s, p):
        return remote(z_ref(origin(d, s), p), zs.at[d, s, p], zr.at[d, s, p], z_next[d])

    def x_send(d, s, p):
        return remote(part(xl, origin(d, s), c, p), xs.at[d, s, p], xr.at[d, s, p], x_dev)

    def x_recv(d, s, p):
        return remote(part(1 - xl, origin(d, s), c, p), xs.at[d, s, p], xr.at[d, s, p], x_dev)

    def c_send(d, s, k):
        return remote(whole((xl + k) % 2, origin(d, s), c), cs.at[d, s, k], cr.at[d, s, k], c_dev)

    def c_recv(d, s, k):
        return remote(whole((xl + k) % 2, origin(d, s), 1 - c), cs.at[d, s, k], cr.at[d, s, k], c_dev)

    def multiply(s):
        zc = jnp.where((z + s) % 2 == 1, (z + s) % NZ, (z - s + NZ) % NZ) // 2
        for half in range(2):
            unit = half * (NZ // 2) + zc
            rows = wbuf[pl.ds(unit * 4, 4)].reshape(4 * w_ref.shape[0], w_ref.shape[1])
            cols = pl.ds(pl.multiple_of(unit * (4 * w_ref.shape[0]), 128), 4 * w_ref.shape[0])
            acc[...] += jnp.dot(x_ref[:, cols], rows, preferred_element_type=jnp.float32)

    wbuf[xl * (2 * NZ) + z * 2 + c] = w_ref[...]
    for p in range(3):
        x_send(0, 0, p).start()
    for p in range(1, 4):
        for d in range(2):
            z_send(d, 1, p).start()
    c_send(0, 0, 0).start()
    acc[...] = jnp.zeros_like(acc)
    x_recv(0, 0, 0).wait_recv()
    for d in range(2):
        z_send(d, 1, 0).start()
    x_recv(0, 0, 1).wait_recv()
    x_recv(0, 0, 2).wait_recv()
    c_send(0, 0, 1).start()

    order = (1, 2, 3, 0)
    last = {0: 0, 1: 0, 2: 1, 3: 1}

    def step(s, carry):
        for p in order:
            for d in range(2):
                z_recv(d, s, p).wait_recv()
                if last[p] == d:
                    z_send(d, s + 1, p).start()
                else:
                    @pl.when(s < NZ // 2 - 1)
                    def _():
                        z_send(d, s + 1, p).start()
                if p >= 2:
                    x_send(d, s, p - 1).start()
        for d in range(2):
            c_send(d, s, 0).start()

        @pl.when(s == 1)
        def _():
            for k in range(2):
                c_recv(0, 0, k).wait_recv()

        @pl.when(s > 1)
        def _():
            for d in range(2):
                for k in range(2):
                    c_recv(d, s - 1, k).wait_recv()
            multiply(s - 1)

        for d in range(2):
            x_recv(d, s, 1).wait_recv()
            x_recv(d, s, 2).wait_recv()
            c_send(d, s, 1).start()
        return carry

    lax.fori_loop(1, NZ // 2, step, 0)
    far = NZ // 2
    for p in order:
        z_recv(last[p], far, p).wait_recv()
        if p >= 2:
            x_send(0, far, p - 1).start()
    c_send(0, far, 0).start()
    for d in range(2):
        for k in range(2):
            c_recv(d, far - 1, k).wait_recv()
    multiply(far - 1)
    x_recv(0, far, 1).wait_recv()
    x_recv(0, far, 2).wait_recv()
    c_send(0, far, 1).start()
    for k in range(2):
        c_recv(0, far, k).wait_recv()
    multiply(far)

    qkv[...] = acc[...].astype(jnp.bfloat16)
    allowed = (idc_ref[...] == idr_ref[...]) & (idr_ref[...] >= 0)
    live = (idc_ref[...] >= 0).astype(jnp.float32)
    for h in range(heads):
        at = [slice(i * width + h * HD, i * width + (h + 1) * HD) for i in range(3)]
        attended, *grads = attend_head(
            qkv[:, at[0]], qkv[:, at[1]], qkv[:, at[2]], g_ref[:, h * HD : (h + 1) * HD], allowed, live
        )
        att_ref[:, h * HD : (h + 1) * HD] = attended
        for i in range(3):
            gbuf[:, at[i]] = grads[i]

    blocks = wbuf.shape[0] // 8
    depth = blocks * w_ref.shape[0]

    def dest(i):
        k = i // 2
        dy = jnp.where(k < 2, k + 2, 3 - k)
        return ((y + dy) % NY) * 2 + (xh + 1 - i % 2) % 2

    def source_free(i):
        return pltpu.make_async_remote_copy(
            src_ref=sbuf.at[i], dst_ref=rbuf.at[i], send_sem=ts.at[i], recv_sem=tr.at[i],
            device_id=(dp, dest(i)), device_id_type=MESH,
        )

    def backward(i, carry):
        rows = wbuf[pl.ds(dest(i) * blocks, blocks)].reshape(depth, w_ref.shape[1])
        sbuf[i] = lax.dot_general(
            gbuf[...], rows, (((1,), (1,)), ((), ())), preferred_element_type=jnp.float32
        ).astype(jnp.bfloat16)

        @pl.when(i < 7)
        def _():
            source_free(i).start()

        return carry

    lax.fori_loop(0, 8, backward, 0)

    for p in range(3):
        x_send(0, 0, p).wait_send()
    for k in range(2):
        c_send(0, 0, k).wait_send()

    def drain(s, carry):
        for d in range(2):
            for p in range(4):
                z_send(d, s, p).wait_send()
            for p in (1, 2):
                x_send(d, s, p).wait_send()
            for k in range(2):
                c_send(d, s, k).wait_send()
        return carry

    lax.fori_loop(1, NZ // 2, drain, 0)
    for p in range(4):
        z_send(last[p], far, p).wait_send()
    for p in (1, 2):
        x_send(0, far, p).wait_send()
    for k in range(2):
        c_send(0, far, k).wait_send()

    total = sbuf[7].astype(jnp.float32)
    for i in range(7):
        source_free(i).wait_recv()
        total += rbuf[i].astype(jnp.float32)
    out_ref[...] = total.astype(jnp.bfloat16)
    for i in range(7):
        source_free(i).wait_send()


def local(patches, qkv_weight, out_grad, image_starts):
    rows, model = patches.shape
    share = qkv_weight.shape[0]
    columns = qkv_weight.shape[1] * qkv_weight.shape[2]
    n_dp = model // share
    ids = lax.dynamic_index_in_dim(image_starts, lax.axis_index("dp"), 0, keepdims=False)
    vmem = pl.BlockSpec(memory_space=pltpu.VMEM)
    bf = jnp.bfloat16
    dma = pltpu.SemaphoreType.DMA
    steps = NZ // 2 + 1
    return pl.pallas_call(
        kernel,
        out_shape=(
            jax.ShapeDtypeStruct(out_grad.shape, bf),
            jax.ShapeDtypeStruct((rows, model // 8), bf),
        ),
        in_specs=[vmem] * 5,
        out_specs=(vmem, vmem),
        scratch_shapes=[
            pltpu.VMEM((n_dp, share, columns), bf),
            pltpu.VMEM((rows, columns), jnp.float32),
            pltpu.VMEM((rows, columns), bf),
            pltpu.VMEM((rows, columns), bf),
            pltpu.VMEM((8, rows, model // 8), bf),
            pltpu.VMEM((7, rows, model // 8), bf),
            dma((2, steps, 4)),
            dma((2, steps, 4)),
            dma((2, steps, 3)),
            dma((2, steps, 3)),
            dma((2, steps, 2)),
            dma((2, steps, 2)),
            dma((8,)),
            dma((8,)),
        ],
        compiler_params=pltpu.CompilerParams(
            collective_id=0, has_side_effects=True, vmem_limit_bytes=56 * 1024 * 1024
        ),
    )(patches, qkv_weight.reshape(share, columns), out_grad, ids[:, None], ids[None, :])


def solution(mesh):
    in_specs = (P("dp", None), P("dp", None, "tensor"), P("dp", "tensor"), P())
    out_specs = (P("dp", "tensor"), P("dp", "tensor"))
    return jax.shard_map(local, mesh=mesh, in_specs=in_specs, out_specs=out_specs, check_vma=False)
```

```python
import functools

import jax
import jax.numpy as jnp
from jax import lax
from jax.experimental import pallas as pl
from jax.experimental.pallas import tpu as pltpu
from jax.sharding import PartitionSpec as P

HD = 128
NZ = 16
NY = 4
UNIT = 16
CAP = 160
MOVE = 64
BASE = CAP - MOVE
MESH = pl.DeviceIdType.MESH


def attend_head(query, key, value, grad_out, allowed, live):
    score_scale = HD ** (-0.5)
    nt = (((1,), (1,)), ((), ()))
    tn = (((0,), (0,)), ((), ()))
    scores = lax.dot_general(query, key, nt, preferred_element_type=jnp.float32) * score_scale
    logits = jnp.where(allowed, scores, -1e30)
    top_score = jnp.max(logits, axis=-1, keepdims=True)
    expo = jnp.exp(logits - top_score)
    probs = expo / jnp.sum(expo, axis=-1, keepdims=True) * live
    low = probs.astype(jnp.bfloat16)
    attended = jnp.dot(low, value, preferred_element_type=jnp.float32).astype(jnp.bfloat16)
    grad_probs = lax.dot_general(grad_out, value, nt, preferred_element_type=jnp.float32)
    grad_value = lax.dot_general(low, grad_out, tn, preferred_element_type=jnp.float32).astype(jnp.bfloat16)
    row_delta = jnp.sum(probs * grad_probs, axis=-1, keepdims=True)
    grad_scores = (probs * (grad_probs - row_delta) * score_scale).astype(jnp.bfloat16)
    grad_query = jnp.dot(grad_scores, key, preferred_element_type=jnp.float32).astype(jnp.bfloat16)
    grad_key = lax.dot_general(grad_scores, query, tn, preferred_element_type=jnp.float32).astype(jnp.bfloat16)
    return attended, grad_query, grad_key, grad_value


def column(ids_ref, shard):
    row = ids_ref[pl.ds(shard, 1), :].astype(jnp.float32)
    return jnp.broadcast_to(row, (HD, row.shape[1])).T


def units(rows, first):
    return [rows[first + at : first + at + UNIT] for at in range(0, MOVE, UNIT)]


def pick(mask, there, other):
    kept = jnp.where(mask, there.astype(jnp.float32), other.astype(jnp.float32) if other is not None else 0.0)
    return kept.astype(there.dtype)


def kernel(
    x_ref, w_ref, g_ref, ids_ref, att_ref, out_ref,
    wbuf, acc, qkv, gbuf, sbuf, rbuf, xw, mbuf, gw, gm, attw, am, outw, om,
    zs, zr, xs, xr, cs, cr, ts, tr, ms, mr, ps, pr, lsem,
):
    dp, t = lax.axis_index("dp"), lax.axis_index("tensor")
    xl, z, c = dp // (2 * NZ), (dp // 2) % NZ, dp % 2
    y, xh = t // 2, t % 2
    share, width = w_ref.shape[1:]
    slot = g_ref.shape[0]
    quarter = xw.shape[1] // NY
    heads = width // HD

    def dev(xl_, z_, c_):
        return (xl_ * (2 * NZ) + z_ * 2 + c_, t)

    z_next = (dev(xl, (z + 1) % NZ, c), dev(xl, (z + NZ - 1) % NZ, c))
    x_dev = dev(1 - xl, z, c)
    c_dev = dev(xl, z, 1 - c)
    cross = (dev(1 - xl, z, c)[0], y * 2 + 1 - xh)
    peers = [(dp, ((y + j // 2) % NY) * 2 + (xh + j) % 2) for j in range(1, 8)]

    barrier = pltpu.get_barrier_semaphore()
    everyone = [*z_next, x_dev, c_dev, cross, *peers]
    for other in everyone:
        pl.semaphore_signal(barrier, inc=1, device_id=other, device_id_type=MESH)
    pl.semaphore_wait(barrier, len(everyone))

    def origin(d, s):
        return (z - s + NZ) % NZ if d == 0 else (z + s) % NZ

    def part(xl_, z_, c_, p):
        return wbuf.at[xl_ * (2 * NZ) + z_ * 2 + c_, p]

    def whole(xl_, z_, c_):
        return wbuf.at[xl_ * (2 * NZ) + z_ * 2 + c_]

    def z_ref(zo, p):
        return part(1 - xl, zo, c, 0) if p == 0 else part(xl, zo, c, p - 1)

    def remote(ref, send, recv, device):
        return pltpu.make_async_remote_copy(
            src_ref=ref, dst_ref=ref, send_sem=send, recv_sem=recv, device_id=device, device_id_type=MESH
        )

    def z_send(d, s, p):
        return remote(z_ref(origin(d, s - 1), p), zs.at[d, s, p], zr.at[d, s, p], z_next[d])

    def z_recv(d, s, p):
        return remote(z_ref(origin(d, s), p), zs.at[d, s, p], zr.at[d, s, p], z_next[d])

    def x_send(d, s, p):
        return remote(part(xl, origin(d, s), c, p), xs.at[d, s, p], xr.at[d, s, p], x_dev)

    def x_recv(d, s, p):
        return remote(part(1 - xl, origin(d, s), c, p), xs.at[d, s, p], xr.at[d, s, p], x_dev)

    def c_send(d, s, k):
        return remote(whole((xl + k) % 2, origin(d, s), c), cs.at[d, s, k], cr.at[d, s, k], c_dev)

    def c_recv(d, s, k):
        return remote(whole((xl + k) % 2, origin(d, s), 1 - c), cs.at[d, s, k], cr.at[d, s, k], c_dev)

    def weight_rows(first, count):
        return jnp.concatenate(
            [wbuf[pl.ds(first, count), p].reshape(count * share, width) for p in range(3)], axis=1
        )

    def multiply(s):
        zc = jnp.where((z + s) % 2 == 1, (z + s) % NZ, (z - s + NZ) % NZ) // 2
        for half in range(2):
            unit = half * (NZ // 2) + zc
            cols = pl.ds(pl.multiple_of(unit * (4 * share), 128), 4 * share)
            acc[...] += jnp.dot(xw[:, cols], weight_rows(unit * 4, 4), preferred_element_type=jnp.float32)

    def move_copy(k, quarter_at, device):
        ref = mbuf.at[quarter_at]
        cols = pl.ds(pl.multiple_of(y * quarter, HD), quarter)
        src = x_ref.at[pl.ds(CAP, MOVE), cols] if k == 0 else ref
        return pltpu.make_async_remote_copy(
            src_ref=src, dst_ref=ref, send_sem=ms.at[k], recv_sem=mr.at[k], device_id=device, device_id_type=MESH
        )

    def move_send(k):
        return move_copy(k, y, cross if k == 0 else (dp, ((y + k) % NY) * 2 + xh))

    def move_recv(k):
        return move_copy(k, (y - k + NY) % NY, cross)

    def swap(k, src, dst):
        return pltpu.make_async_remote_copy(
            src_ref=src, dst_ref=dst, send_sem=ps.at[k], recv_sem=pr.at[k], device_id=x_dev, device_id_type=MESH
        )

    grads_swap = swap(0, g_ref.at[pl.ds(CAP, MOVE)], gm)
    att_swap = swap(1, attw.at[pl.ds(BASE, MOVE)], am)
    out_swap = swap(2, outw, om)
    own_rows = pltpu.make_async_copy(x_ref.at[pl.ds(0, CAP)], xw, lsem)

    own_rows.start()
    wbuf[xl * (2 * NZ) + z * 2 + c] = w_ref[...]
    for p in range(3):
        x_send(0, 0, p).start()
    for p in range(1, 4):
        for d in range(2):
            z_send(d, 1, p).start()
    c_send(0, 0, 0).start()
    move_send(0).start()
    acc[...] = jnp.zeros_like(acc)
    own_ids = column(ids_ref, dp)
    other_ids = column(ids_ref, dev(1 - xl, z, c)[0])
    own_live = own_ids[:, :1] >= 0.0
    taken = [
        jnp.where(own >= 0.0, own, other)
        for own, other in zip(units(own_ids, BASE), units(other_ids, CAP)[::-1], strict=True)
    ]
    work_ids = jnp.concatenate([own_ids[:BASE], *taken], axis=0)

    def fill():
        for k in range(1, NY):
            move_recv(k).wait_recv()
        own_rows.wait()
        for at in range(MOVE // UNIT):
            mask = own_live[BASE + at * UNIT : BASE + (at + 1) * UNIT]
            rows = pl.ds(BASE + at * UNIT, UNIT)
            back = pl.ds(MOVE - (at + 1) * UNIT, UNIT)
            for q in range(NY):
                cols = pl.ds(q * quarter, quarter)
                xw[rows, cols] = pick(mask, xw[rows, cols], mbuf[q, back, :])

    x_recv(0, 0, 0).wait_recv()
    for d in range(2):
        z_send(d, 1, 0).start()
    x_recv(0, 0, 1).wait_recv()
    x_recv(0, 0, 2).wait_recv()
    c_send(0, 0, 1).start()

    order = (2, 3, 1, 0)
    last = {0: 0, 1: 0, 2: 1, 3: 1}
    far = NZ // 2

    def pass_x(d, s):
        x_recv(d, s, 1).wait_recv()
        x_recv(d, s, 2).wait_recv()
        c_send(d, s, 1).start()

    def use(ds, s):
        for d in ds:
            for k in range(2):
                c_recv(d, s, k).wait_recv()
        multiply(s)

    def step(s, carry):
        for p in order:
            for d in range(2):
                z_recv(d, s, p).wait_recv()
                if last[p] == d:
                    z_send(d, s + 1, p).start()
                else:
                    @pl.when(s < far - 1)
                    def _():
                        z_send(d, s + 1, p).start()
                if p >= 2:
                    x_send(d, s, p - 1).start()
        for d in range(2):
            c_send(d, s, 0).start()

        @pl.when(s == 1)
        def _():
            for k in range(2):
                c_recv(0, 0, k).wait_recv()
            move_recv(0).wait_recv()
            for k in range(1, NY):
                move_send(k).start()
            grads_swap.start()

        @pl.when(s > 1)
        def _():
            for d in range(2):
                pass_x(d, s - 1)

        @pl.when(s == 3)
        def _():
            fill()

        @pl.when(s > 2)
        def _():
            use((0, 1), s - 2)

        return carry

    lax.fori_loop(1, far, step, 0)
    for p in order:
        z_recv(last[p], far, p).wait_recv()
        if p >= 2:
            x_send(0, far, p - 1).start()
    c_send(0, far, 0).start()
    for d in range(2):
        pass_x(d, far - 1)
    use((0, 1), far - 2)
    pass_x(0, far)
    use((0, 1), far - 1)
    use((0,), far)

    qkv[...] = acc[...].astype(jnp.bfloat16)
    row_ids = work_ids.T[:1]
    allowed = (work_ids[:, :1] == row_ids) & (row_ids >= 0.0)
    live = (work_ids[:, :1] >= 0.0).astype(jnp.float32)
    grads_swap.wait_recv()
    gw[pl.ds(0, BASE)] = g_ref[pl.ds(0, BASE)]
    for at in range(MOVE // UNIT):
        rows = pl.ds(BASE + at * UNIT, UNIT)
        mask = own_live[BASE + at * UNIT : BASE + (at + 1) * UNIT]
        gw[rows] = pick(mask, g_ref[rows], gm[pl.ds(MOVE - (at + 1) * UNIT, UNIT)])
    for h in range(heads):
        at = [slice(i * width + h * HD, i * width + (h + 1) * HD) for i in range(3)]
        attended, *grads = attend_head(
            qkv[:, at[0]], qkv[:, at[1]], qkv[:, at[2]], gw[:, h * HD : (h + 1) * HD], allowed, live
        )
        attw[:, h * HD : (h + 1) * HD] = attended
        for i in range(3):
            gbuf[:, at[i]] = grads[i]

    att_swap.start()

    blocks = wbuf.shape[0] // 8

    def dest(i):
        k = i // 2
        dy = jnp.where(k < 2, k + 2, 3 - k)
        return ((y + dy) % NY) * 2 + (xh + 1 - i % 2) % 2

    parts = (pl.ds(BASE, MOVE), pl.ds(0, BASE))

    def sums(i, b):
        return pltpu.make_async_remote_copy(
            src_ref=sbuf.at[i, parts[b]], dst_ref=rbuf.at[i, parts[b]], send_sem=ts.at[b, i], recv_sem=tr.at[b, i],
            device_id=(dp, dest(i)), device_id_type=MESH,
        )

    def backward(i, carry):
        rows = weight_rows(dest(i) * blocks, blocks)
        sbuf[i] = lax.dot_general(
            gbuf[...], rows, (((1,), (1,)), ((), ())), preferred_element_type=jnp.float32
        ).astype(jnp.bfloat16)

        @pl.when(i < 7)
        def _():
            sums(i, 0).start()

        return carry

    lax.fori_loop(0, 8, backward, 0)

    def rest(i, carry):
        sums(i, 1).start()
        return carry

    lax.fori_loop(0, 7, rest, 0)

    for p in range(3):
        x_send(0, 0, p).wait_send()
    for k in range(2):
        c_send(0, 0, k).wait_send()

    def drain(s, carry):
        for d in range(2):
            for p in range(4):
                z_send(d, s, p).wait_send()
            for p in (1, 2):
                x_send(d, s, p).wait_send()
            for k in range(2):
                c_send(d, s, k).wait_send()
        return carry

    lax.fori_loop(1, NZ // 2, drain, 0)
    for p in range(4):
        z_send(last[p], far, p).wait_send()
    for p in (1, 2):
        x_send(0, far, p).wait_send()
    for k in range(2):
        c_send(0, far, k).wait_send()

    for k in range(NY):
        move_send(k).wait_send()
    grads_swap.wait_send()

    def give(ref, work, received):
        for at in range(MOVE // UNIT):
            for first, rows, index in ((BASE, work, at), (CAP, received, MOVE // UNIT - 1 - at)):
                here = first + at * UNIT
                if rows is not None:
                    mask = own_live[here : here + UNIT]
                    ref[pl.ds(here, UNIT)] = pick(mask, rows[pl.ds(index * UNIT, UNIT)], None)

    att_ref[pl.ds(0, BASE)] = attw[pl.ds(0, BASE)]
    att_swap.wait()
    give(att_ref, attw.at[pl.ds(BASE, MOVE)], am)

    def added(b):
        total = sbuf[7, parts[b]].astype(jnp.float32)
        for i in range(7):
            sums(i, b).wait_recv()
            total += rbuf[i, parts[b]].astype(jnp.float32)
        return total.astype(jnp.bfloat16)

    outw[...] = added(0)
    out_swap.start()
    give(out_ref, outw, None)
    out_ref[pl.ds(0, BASE)] = added(1)
    out_swap.wait()
    give(out_ref, None, om)
    for b in range(2):
        for i in range(7):
            sums(i, b).wait_send()


def local(patches, qkv_weight, out_grad, image_starts):
    rows, model = patches.shape
    share = qkv_weight.shape[0]
    columns = qkv_weight.shape[1] * qkv_weight.shape[2]
    n_dp = model // share
    vmem = pl.BlockSpec(memory_space=pltpu.VMEM)
    bf = jnp.bfloat16
    dma = pltpu.SemaphoreType.DMA
    steps = NZ // 2 + 1
    return pl.pallas_call(
        kernel,
        out_shape=(
            jax.ShapeDtypeStruct(out_grad.shape, bf),
            jax.ShapeDtypeStruct((rows, model // 8), bf),
        ),
        in_specs=[pl.BlockSpec(memory_space=pl.ANY), vmem, vmem, vmem],
        out_specs=(vmem, vmem),
        scratch_shapes=[
            pltpu.VMEM((n_dp, 3, share, columns // 3), bf),
            pltpu.VMEM((CAP, columns), jnp.float32),
            pltpu.VMEM((CAP, columns), bf),
            pltpu.VMEM((CAP, columns), bf),
            pltpu.VMEM((8, CAP, model // 8), bf),
            pltpu.VMEM((7, CAP, model // 8), bf),
            pltpu.VMEM((CAP, model), bf),
            pltpu.VMEM((NY, MOVE, model // NY), bf),
            pltpu.VMEM((CAP, columns // 3), bf),
            pltpu.VMEM((MOVE, columns // 3), bf),
            pltpu.VMEM((CAP, columns // 3), bf),
            pltpu.VMEM((MOVE, columns // 3), bf),
            pltpu.VMEM((MOVE, model // 8), bf),
            pltpu.VMEM((MOVE, model // 8), bf),
            dma((2, steps, 4)),
            dma((2, steps, 4)),
            dma((2, steps, 3)),
            dma((2, steps, 3)),
            dma((2, steps, 2)),
            dma((2, steps, 2)),
            dma((2, 8)),
            dma((2, 8)),
            dma((NY,)),
            dma((NY,)),
            dma((3,)),
            dma((3,)),
            dma(()),
        ],
        compiler_params=pltpu.CompilerParams(
            collective_id=0, has_side_effects=True, vmem_limit_bytes=56 * 1024 * 1024
        ),
    )(patches, qkv_weight.transpose(1, 0, 2), out_grad, image_starts)


def solution(mesh):
    in_specs = (P("dp", None), P("dp", None, "tensor"), P("dp", "tensor"), P())
    out_specs = (P("dp", "tensor"), P("dp", "tensor"))
    return jax.shard_map(local, mesh=mesh, in_specs=in_specs, out_specs=out_specs, check_vma=False)
```

```python
import functools

import jax
import jax.numpy as jnp
from jax import lax
from jax.experimental import pallas as pl
from jax.experimental.pallas import tpu as pltpu
from jax.sharding import PartitionSpec as P

HD = 128
NZ = 16
NY = 4
UNIT = 16
CAP = 160
MOVE = 64
BASE = CAP - MOVE
EARLY = 32
MESH = pl.DeviceIdType.MESH


def attend_head(query, key, value, grad_out, allowed, live):
    score_scale = HD ** (-0.5)
    nt = (((1,), (1,)), ((), ()))
    tn = (((0,), (0,)), ((), ()))
    scores = lax.dot_general(query, key, nt, preferred_element_type=jnp.float32) * score_scale
    logits = jnp.where(allowed, scores, -1e30)
    top_score = jnp.max(logits, axis=-1, keepdims=True)
    expo = jnp.exp(logits - top_score)
    probs = expo / jnp.sum(expo, axis=-1, keepdims=True) * live
    low = probs.astype(jnp.bfloat16)
    attended = jnp.dot(low, value, preferred_element_type=jnp.float32).astype(jnp.bfloat16)
    grad_probs = lax.dot_general(grad_out, value, nt, preferred_element_type=jnp.float32)
    grad_value = lax.dot_general(low, grad_out, tn, preferred_element_type=jnp.float32).astype(jnp.bfloat16)
    row_delta = jnp.sum(probs * grad_probs, axis=-1, keepdims=True)
    grad_scores = (probs * (grad_probs - row_delta) * score_scale).astype(jnp.bfloat16)
    grad_query = jnp.dot(grad_scores, key, preferred_element_type=jnp.float32).astype(jnp.bfloat16)
    grad_key = lax.dot_general(grad_scores, query, tn, preferred_element_type=jnp.float32).astype(jnp.bfloat16)
    return attended, grad_query, grad_key, grad_value


def column(ids_ref, shard):
    row = ids_ref[pl.ds(shard, 1), :].astype(jnp.float32)
    return jnp.broadcast_to(row, (HD, row.shape[1])).T


def units(rows, first):
    return [rows[first + at : first + at + UNIT] for at in range(0, MOVE, UNIT)]


def pick(mask, there, other):
    kept = jnp.where(mask, there.astype(jnp.float32), other.astype(jnp.float32) if other is not None else 0.0)
    return kept.astype(there.dtype)


def kernel(
    x_ref, w_ref, g_ref, ids_ref, att_ref, out_ref,
    wbuf, acc, qkv, gbuf, sbuf, rbuf, xw, mbuf, wrem, grem, gs, gw, gm, attw, am, ats, arem, outw, om,
    zs, zr, xs, xr, cs, cr, ts, tr, ms, mr, ps, pr, bs, br, lsem,
):
    dp, t = lax.axis_index("dp"), lax.axis_index("tensor")
    xl, z, c = dp // (2 * NZ), (dp // 2) % NZ, dp % 2
    y, xh = t // 2, t % 2
    share, width = w_ref.shape[1:]
    b_own = dp
    quarter = xw.shape[1] // NY
    heads = width // HD

    def dev(xl_, z_, c_):
        return (xl_ * (2 * NZ) + z_ * 2 + c_, t)

    z_next = (dev(xl, (z + 1) % NZ, c), dev(xl, (z + NZ - 1) % NZ, c))
    x_dev = dev(1 - xl, z, c)
    c_dev = dev(xl, z, 1 - c)
    cross = (dev(1 - xl, z, c)[0], y * 2 + 1 - xh)
    sib = (dp, y * 2 + 1 - xh)
    peers = [(dp, ((y + j // 2) % NY) * 2 + (xh + j) % 2) for j in range(1, 8)]

    barrier = pltpu.get_barrier_semaphore()
    everyone = [*z_next, x_dev, c_dev, cross, *peers]
    for other in everyone:
        pl.semaphore_signal(barrier, inc=1, device_id=other, device_id_type=MESH)
    pl.semaphore_wait(barrier, len(everyone))

    def origin(d, s):
        return (z - s + NZ) % NZ if d == 0 else (z + s) % NZ

    def block(xl_, z_, c_):
        return xl_ * (2 * NZ) + z_ * 2 + c_

    def x_ref_part(xl_, zo, p):
        at = block(xl_, zo, c)
        if p == 0:
            return wbuf.at[at, 0, :, pl.ds(EARLY, share - EARLY), :]
        return wbuf.at[at, 0, :, pl.ds(0, EARLY), :] if p == 3 else wbuf.at[at, p]

    def whole(xl_, z_, c_):
        return wbuf.at[block(xl_, z_, c_)]

    def z_ref(zo, p):
        return x_ref_part(1 - xl, zo, 3) if p == 0 else wbuf.at[block(xl, zo, c), p - 1]

    def remote(ref, send, recv, device):
        return pltpu.make_async_remote_copy(
            src_ref=ref, dst_ref=ref, send_sem=send, recv_sem=recv, device_id=device, device_id_type=MESH
        )

    def z_send(d, s, p):
        return remote(z_ref(origin(d, s - 1), p), zs.at[d, s, p], zr.at[d, s, p], z_next[d])

    def z_recv(d, s, p):
        return remote(z_ref(origin(d, s), p), zs.at[d, s, p], zr.at[d, s, p], z_next[d])

    def x_send(d, s, p):
        return remote(x_ref_part(xl, origin(d, s), p), xs.at[d, s, p], xr.at[d, s, p], cross if p == 2 else x_dev)

    def x_recv(d, s, p):
        return remote(x_ref_part(1 - xl, origin(d, s), p), xs.at[d, s, p], xr.at[d, s, p], cross if p == 2 else x_dev)

    def c_send(d, s, k):
        return remote(whole((xl + k) % 2, origin(d, s), c), cs.at[d, s, k], cr.at[d, s, k], c_dev)

    def c_recv(d, s, k):
        return remote(whole((xl + k) % 2, origin(d, s), 1 - c), cs.at[d, s, k], cr.at[d, s, k], c_dev)

    def weight_rows(first, count):
        return jnp.concatenate(
            [
                wbuf[pl.ds(first, count), j, i].reshape(count * share, HD)
                for i in range(3)
                for j in range(heads)
            ],
            axis=1,
        )

    def multiply(s):
        zc = jnp.where((z + s) % 2 == 1, (z + s) % NZ, (z - s + NZ) % NZ) // 2
        for half in range(2):
            unit = half * (NZ // 2) + zc
            cols = pl.ds(pl.multiple_of(unit * (4 * share), 128), 4 * share)
            acc[...] += jnp.dot(xw[:, cols], weight_rows(unit * 4, 4), preferred_element_type=jnp.float32)

    def move_copy(k, quarter_at, device):
        ref = mbuf.at[quarter_at]
        cols = pl.ds(pl.multiple_of(y * quarter, HD), quarter)
        src = x_ref.at[pl.ds(CAP, MOVE), cols] if k == 0 else ref
        return pltpu.make_async_remote_copy(
            src_ref=src, dst_ref=ref, send_sem=ms.at[k], recv_sem=mr.at[k], device_id=device, device_id_type=MESH
        )

    def move_send(k):
        return move_copy(k, y, cross if k == 0 else (dp, ((y + k) % NY) * 2 + xh))

    def move_recv(k):
        return move_copy(k, (y - k + NY) % NY, cross)

    def swap(k, src, dst, device):
        return pltpu.make_async_remote_copy(
            src_ref=src, dst_ref=dst, send_sem=ps.at[k], recv_sem=pr.at[k], device_id=device, device_id_type=MESH
        )

    def with_sib(k, src, dst):
        return pltpu.make_async_remote_copy(
            src_ref=src, dst_ref=dst, send_sem=bs.at[k], recv_sem=br.at[k], device_id=sib, device_id_type=MESH
        )

    pair, lone = pl.ds(0, 2), pl.ds(2, 1)
    moved, tail = pl.ds(CAP, MOVE), pl.ds(BASE, MOVE)
    grads_swaps = (
        swap(0, gs.at[pair, moved], gm.at[pair], x_dev),
        swap(1, gs.at[lone, moved], gm.at[lone], cross),
    )
    att_swaps = (
        swap(2, attw.at[pair, tail], am.at[pair], x_dev),
        swap(3, attw.at[lone, tail], am.at[lone], cross),
    )
    out_swap = swap(4, outw, om, x_dev)
    weight_sib = with_sib(0, wrem, wbuf.at[b_own, 2])
    grads_sib = with_sib(1, grem, gs.at[2])
    att_sib = with_sib(2, ats.at[2], arem)

    def head(k):
        return pl.ds(pl.multiple_of(k * HD, HD), HD)

    kept = (head(xh), head(xh + 1))
    spare = head(2 - 2 * xh)
    same = xl == 0
    own_rows = pltpu.make_async_copy(x_ref.at[pl.ds(0, CAP)], xw, lsem)

    own_rows.start()
    for i in range(3):
        wrem[i] = w_ref[i, :, spare]

    @pl.when(xl == 1)
    def _():
        weight_sib.start()

    for j in range(2):
        for i in range(3):
            wbuf[b_own, j, i] = w_ref[i, :, kept[j]]
    for p in (3, 0, 1):
        x_send(0, 0, p).start()
    for p in (1, 2):
        for d in range(2):
            z_send(d, 1, p).start()

    @pl.when(same)
    def _():
        wbuf[b_own, 2] = wrem[...]

    grem[...] = g_ref[:, spare]
    for j in range(2):
        gs[j] = g_ref[:, kept[j]]

    @pl.when(same)
    def _():
        gs[2] = grem[...]

    @pl.when(xl == 1)
    def _():
        grads_sib.start()
        weight_sib.wait_recv()

    x_send(0, 0, 2).start()
    for d in range(2):
        z_send(d, 1, 3).start()
    c_send(0, 0, 0).start()
    x_recv(0, 0, 3).wait_recv()
    for d in range(2):
        z_send(d, 1, 0).start()
    move_send(0).start()
    acc[...] = jnp.zeros_like(acc)
    own_ids = column(ids_ref, dp)
    other_ids = column(ids_ref, dev(1 - xl, z, c)[0])
    own_live = own_ids[:, :1] >= 0.0
    taken = [
        jnp.where(own >= 0.0, own, other)
        for own, other in zip(units(own_ids, BASE), units(other_ids, CAP)[::-1], strict=True)
    ]
    work_ids = jnp.concatenate([own_ids[:BASE], *taken], axis=0)

    def fill():
        for k in range(1, NY):
            move_recv(k).wait_recv()
        own_rows.wait()
        for at in range(MOVE // UNIT):
            mask = own_live[BASE + at * UNIT : BASE + (at + 1) * UNIT]
            rows = pl.ds(BASE + at * UNIT, UNIT)
            back = pl.ds(MOVE - (at + 1) * UNIT, UNIT)
            for q in range(NY):
                cols = pl.ds(q * quarter, quarter)
                xw[rows, cols] = pick(mask, xw[rows, cols], mbuf[q, back, :])

    for p in range(3):
        x_recv(0, 0, p).wait_recv()
    c_send(0, 0, 1).start()

    order = (1, 2, 3, 0)
    last = {1: 0, 2: 0, 3: 1, 0: 1}
    far = NZ // 2

    def pass_x(d, s):
        for p in range(3):
            x_recv(d, s, p).wait_recv()
        c_send(d, s, 1).start()

    def use(ds, s):
        for d in ds:
            for k in range(2):
                c_recv(d, s, k).wait_recv()
        multiply(s)

    def step(s, carry):
        for p in order:
            for d in range(2):
                z_recv(d, s, p).wait_recv()
                if last[p] == d:
                    z_send(d, s + 1, p).start()
                else:
                    @pl.when(s < far - 1)
                    def _():
                        z_send(d, s + 1, p).start()
                if p >= 1:
                    x_send(d, s, p - 1).start()
        for d in range(2):
            c_send(d, s, 0).start()

        @pl.when(s == 1)
        def _():
            for k in range(2):
                c_recv(0, 0, k).wait_recv()
            move_recv(0).wait_recv()
            for k in range(1, NY):
                move_send(k).start()

            @pl.when(xl == 1)
            def _():
                grads_sib.wait_recv()

            for copy in grads_swaps:
                copy.start()

        @pl.when(s > 1)
        def _():
            for d in range(2):
                pass_x(d, s - 1)

        @pl.when(s == 3)
        def _():
            fill()

        @pl.when(s > 2)
        def _():
            use((0, 1), s - 2)

        return carry

    lax.fori_loop(1, far, step, 0)
    for p in order:
        z_recv(last[p], far, p).wait_recv()
        if p >= 1:
            x_send(0, far, p - 1).start()
    c_send(0, far, 0).start()
    for d in range(2):
        pass_x(d, far - 1)
    use((0, 1), far - 2)
    pass_x(0, far)
    use((0, 1), far - 1)
    use((0,), far)

    qkv[...] = acc[...].astype(jnp.bfloat16)
    row_ids = work_ids.T[:1]
    allowed = (work_ids[:, :1] == row_ids) & (row_ids >= 0.0)
    live = (work_ids[:, :1] >= 0.0).astype(jnp.float32)
    for copy in grads_swaps:
        copy.wait_recv()
    for j in range(heads):
        gw[j, pl.ds(0, BASE)] = gs[j, pl.ds(0, BASE)]
        for at in range(MOVE // UNIT):
            rows = pl.ds(BASE + at * UNIT, UNIT)
            mask = own_live[BASE + at * UNIT : BASE + (at + 1) * UNIT]
            gw[j, rows] = pick(mask, gs[j, rows], gm[j, pl.ds(MOVE - (at + 1) * UNIT, UNIT)])
    for h in range(heads):
        at = [slice(i * width + h * HD, i * width + (h + 1) * HD) for i in range(3)]
        attended, *grads = attend_head(
            qkv[:, at[0]], qkv[:, at[1]], qkv[:, at[2]], gw[h], allowed, live
        )
        attw[h] = attended
        for i in range(3):
            gbuf[:, at[i]] = grads[i]

    for copy in att_swaps:
        copy.start()

    blocks = wbuf.shape[0] // 8

    def dest(i):
        k = i // 2
        dy = jnp.where(k < 2, k + 2, 3 - k)
        return ((y + dy) % NY) * 2 + (xh + 1 - i % 2) % 2

    parts = (pl.ds(BASE, MOVE), pl.ds(0, BASE))

    def sums(i, b):
        return pltpu.make_async_remote_copy(
            src_ref=sbuf.at[i, parts[b]], dst_ref=rbuf.at[i, parts[b]], send_sem=ts.at[b, i], recv_sem=tr.at[b, i],
            device_id=(dp, dest(i)), device_id_type=MESH,
        )

    def backward(i, carry):
        rows = weight_rows(dest(i) * blocks, blocks)
        sbuf[i] = lax.dot_general(
            gbuf[...], rows, (((1,), (1,)), ((), ())), preferred_element_type=jnp.float32
        ).astype(jnp.bfloat16)

        @pl.when(i < 7)
        def _():
            sums(i, 0).start()

        return carry

    lax.fori_loop(0, 8, backward, 0)

    def rest(i, carry):
        sums(i, 1).start()
        return carry

    lax.fori_loop(0, 7, rest, 0)

    for p in range(4):
        x_send(0, 0, p).wait_send()
    for k in range(2):
        c_send(0, 0, k).wait_send()

    def drain(s, carry):
        for d in range(2):
            for p in range(4):
                z_send(d, s, p).wait_send()
            for p in range(3):
                x_send(d, s, p).wait_send()
            for k in range(2):
                c_send(d, s, k).wait_send()
        return carry

    lax.fori_loop(1, NZ // 2, drain, 0)
    for p in range(4):
        z_send(last[p], far, p).wait_send()
    for p in range(3):
        x_send(0, far, p).wait_send()
    for k in range(2):
        c_send(0, far, k).wait_send()

    for k in range(NY):
        move_send(k).wait_send()
    for copy in grads_swaps:
        copy.wait_send()

    def give(ref, work, received):
        for at in range(MOVE // UNIT):
            for first, rows, index in ((BASE, work, at), (CAP, received, MOVE // UNIT - 1 - at)):
                here = first + at * UNIT
                if rows is not None:
                    mask = own_live[here : here + UNIT]
                    ref[pl.ds(here, UNIT)] = pick(mask, rows[pl.ds(index * UNIT, UNIT)], None)

    for copy in att_swaps:
        copy.wait()
    for j in range(heads):
        ats[j, pl.ds(0, BASE)] = attw[j, pl.ds(0, BASE)]
        give(ats.at[j], attw.at[j, tail], am.at[j])

    @pl.when(xl == 1)
    def _():
        att_sib.start()
        weight_sib.wait_send()
        grads_sib.wait_send()

    for j in range(2):
        att_ref[:, kept[j]] = ats[j]

    @pl.when(same)
    def _():
        att_ref[:, spare] = ats[2]

    def added(b):
        total = sbuf[7, parts[b]].astype(jnp.float32)
        for i in range(7):
            sums(i, b).wait_recv()
            total += rbuf[i, parts[b]].astype(jnp.float32)
        return total.astype(jnp.bfloat16)

    outw[...] = added(0)
    out_swap.start()

    @pl.when(xl == 1)
    def _():
        att_sib.wait()
        att_ref[:, spare] = arem[...]

    give(out_ref, outw, None)
    out_ref[pl.ds(0, BASE)] = added(1)
    out_swap.wait()
    give(out_ref, None, om)
    for b in range(2):
        for i in range(7):
            sums(i, b).wait_send()


def local(patches, qkv_weight, out_grad, image_starts):
    rows, model = patches.shape
    share = qkv_weight.shape[0]
    columns = qkv_weight.shape[1] * qkv_weight.shape[2]
    n_dp = model // share
    heads = columns // (3 * HD)
    vmem = pl.BlockSpec(memory_space=pltpu.VMEM)
    bf = jnp.bfloat16
    dma = pltpu.SemaphoreType.DMA
    steps = NZ // 2 + 1
    return pl.pallas_call(
        kernel,
        out_shape=(
            jax.ShapeDtypeStruct(out_grad.shape, bf),
            jax.ShapeDtypeStruct((rows, model // 8), bf),
        ),
        in_specs=[pl.BlockSpec(memory_space=pl.ANY), vmem, vmem, vmem],
        out_specs=(vmem, vmem),
        scratch_shapes=[
            pltpu.VMEM((n_dp, heads, 3, share, HD), bf),
            pltpu.VMEM((CAP, columns), jnp.float32),
            pltpu.VMEM((CAP, columns), bf),
            pltpu.VMEM((CAP, columns), bf),
            pltpu.VMEM((8, CAP, model // 8), bf),
            pltpu.VMEM((7, CAP, model // 8), bf),
            pltpu.VMEM((CAP, model), bf),
            pltpu.VMEM((NY, MOVE, model // NY), bf),
            pltpu.VMEM((3, share, HD), bf),
            pltpu.VMEM((rows, HD), bf),
            pltpu.VMEM((heads, rows, HD), bf),
            pltpu.VMEM((heads, CAP, HD), bf),
            pltpu.VMEM((heads, MOVE, HD), bf),
            pltpu.VMEM((heads, CAP, HD), bf),
            pltpu.VMEM((heads, MOVE, HD), bf),
            pltpu.VMEM((heads, rows, HD), bf),
            pltpu.VMEM((rows, HD), bf),
            pltpu.VMEM((MOVE, model // 8), bf),
            pltpu.VMEM((MOVE, model // 8), bf),
            dma((2, steps, 4)),
            dma((2, steps, 4)),
            dma((2, steps, 4)),
            dma((2, steps, 4)),
            dma((2, steps, 2)),
            dma((2, steps, 2)),
            dma((2, 8)),
            dma((2, 8)),
            dma((NY,)),
            dma((NY,)),
            dma((5,)),
            dma((5,)),
            dma((3,)),
            dma((3,)),
            dma(()),
        ],
        compiler_params=pltpu.CompilerParams(
            collective_id=0, has_side_effects=True, vmem_limit_bytes=56 * 1024 * 1024
        ),
    )(patches, qkv_weight.transpose(1, 0, 2), out_grad, image_starts)


def solution(mesh):
    in_specs = (P("dp", None), P("dp", None, "tensor"), P("dp", "tensor"), P())
    out_specs = (P("dp", "tensor"), P("dp", "tensor"))
    return jax.shard_map(local, mesh=mesh, in_specs=in_specs, out_specs=out_specs, check_vma=False)
```

```python
import functools

import jax
import jax.numpy as jnp
from jax import lax
from jax.experimental import pallas as pl
from jax.experimental.pallas import tpu as pltpu
from jax.sharding import PartitionSpec as P

HD = 128
NZ = 16
NY = 4
UNIT = 16
CAP = 160
MOVE = 64
BASE = CAP - MOVE
EARLY = 32
FILL = 5
MESH = pl.DeviceIdType.MESH


def attend_head(query, key, value, grad_out, allowed, live):
    score_scale = HD ** (-0.5)
    nt = (((1,), (1,)), ((), ()))
    tn = (((0,), (0,)), ((), ()))
    scores = lax.dot_general(query, key, nt, preferred_element_type=jnp.float32) * score_scale
    logits = jnp.where(allowed, scores, -1e30)
    top_score = jnp.max(logits, axis=-1, keepdims=True)
    expo = jnp.exp(logits - top_score)
    probs = expo / jnp.sum(expo, axis=-1, keepdims=True) * live
    low = probs.astype(jnp.bfloat16)
    attended = jnp.dot(low, value, preferred_element_type=jnp.float32).astype(jnp.bfloat16)
    grad_probs = lax.dot_general(grad_out, value, nt, preferred_element_type=jnp.float32)
    grad_value = lax.dot_general(low, grad_out, tn, preferred_element_type=jnp.float32).astype(jnp.bfloat16)
    row_delta = jnp.sum(probs * grad_probs, axis=-1, keepdims=True)
    grad_scores = (probs * (grad_probs - row_delta) * score_scale).astype(jnp.bfloat16)
    grad_query = jnp.dot(grad_scores, key, preferred_element_type=jnp.float32).astype(jnp.bfloat16)
    grad_key = lax.dot_general(grad_scores, query, tn, preferred_element_type=jnp.float32).astype(jnp.bfloat16)
    return attended, grad_query, grad_key, grad_value


def column(ids_ref, shard):
    row = ids_ref[pl.ds(shard, 1), :].astype(jnp.float32)
    return jnp.broadcast_to(row, (HD, row.shape[1])).T


def units(rows, first):
    return [rows[first + at : first + at + UNIT] for at in range(0, MOVE, UNIT)]


def pick(mask, there, other):
    kept = jnp.where(mask, there.astype(jnp.float32), other.astype(jnp.float32) if other is not None else 0.0)
    return kept.astype(there.dtype)


def kernel(
    x_ref, w_ref, g_ref, ids_ref, att_ref, out_ref,
    wbuf, acc, qkv, gbuf, sbuf, rbuf, xw, mbuf, wrem, grem, gs, gw, gm, attw, am, ats, arem, outw, om,
    zs, zr, xs, xr, cs, cr, ts, tr, ms, mr, ps, pr, bs, br, lsem,
):
    dp, t = lax.axis_index("dp"), lax.axis_index("tensor")
    xl, z, c = dp // (2 * NZ), (dp // 2) % NZ, dp % 2
    y, xh = t // 2, t % 2
    share, width = w_ref.shape[1:]
    b_own = dp
    quarter = xw.shape[1] // NY
    heads = width // HD

    def dev(xl_, z_, c_):
        return (xl_ * (2 * NZ) + z_ * 2 + c_, t)

    z_next = (dev(xl, (z + 1) % NZ, c), dev(xl, (z + NZ - 1) % NZ, c))
    x_dev = dev(1 - xl, z, c)
    c_dev = dev(xl, z, 1 - c)
    cross = (dev(1 - xl, z, c)[0], y * 2 + 1 - xh)
    sib = (dp, y * 2 + 1 - xh)
    peers = [(dp, ((y + j // 2) % NY) * 2 + (xh + j) % 2) for j in range(1, 8)]

    barrier = pltpu.get_barrier_semaphore()
    everyone = [*z_next, x_dev, c_dev, cross, *peers]
    for other in everyone:
        pl.semaphore_signal(barrier, inc=1, device_id=other, device_id_type=MESH)

    def origin(d, s):
        return (z - s + NZ) % NZ if d == 0 else (z + s) % NZ

    def block(xl_, z_, c_):
        return xl_ * (2 * NZ) + z_ * 2 + c_

    def x_ref_part(xl_, zo, p):
        at = block(xl_, zo, c)
        if p == 0:
            return wbuf.at[at, 0, :, pl.ds(EARLY, share - EARLY), :]
        return wbuf.at[at, 0, :, pl.ds(0, EARLY), :] if p == 3 else wbuf.at[at, p]

    def whole(xl_, z_, c_):
        return wbuf.at[block(xl_, z_, c_)]

    def z_ref(zo, p):
        return x_ref_part(1 - xl, zo, 3) if p == 0 else wbuf.at[block(xl, zo, c), p - 1]

    def remote(ref, send, recv, device):
        return pltpu.make_async_remote_copy(
            src_ref=ref, dst_ref=ref, send_sem=send, recv_sem=recv, device_id=device, device_id_type=MESH
        )

    def z_send(d, s, p):
        return remote(z_ref(origin(d, s - 1), p), zs.at[d, s, p], zr.at[d, s, p], z_next[d])

    def z_recv(d, s, p):
        return remote(z_ref(origin(d, s), p), zs.at[d, s, p], zr.at[d, s, p], z_next[d])

    def x_send(d, s, p):
        return remote(x_ref_part(xl, origin(d, s), p), xs.at[d, s, p], xr.at[d, s, p], cross if p == 2 else x_dev)

    def x_recv(d, s, p):
        return remote(x_ref_part(1 - xl, origin(d, s), p), xs.at[d, s, p], xr.at[d, s, p], cross if p == 2 else x_dev)

    def c_send(d, s, k):
        return remote(whole((xl + k) % 2, origin(d, s), c), cs.at[d, s, k], cr.at[d, s, k], c_dev)

    def c_recv(d, s, k):
        return remote(whole((xl + k) % 2, origin(d, s), 1 - c), cs.at[d, s, k], cr.at[d, s, k], c_dev)

    def weight_rows(first, count):
        return jnp.concatenate(
            [
                wbuf[pl.ds(first, count), j, i].reshape(count * share, HD)
                for i in range(3)
                for j in range(heads)
            ],
            axis=1,
        )

    def multiply(s):
        zc = jnp.where((z + s) % 2 == 1, (z + s) % NZ, (z - s + NZ) % NZ) // 2
        for half in range(2):
            unit = half * (NZ // 2) + zc
            cols = pl.ds(pl.multiple_of(unit * (4 * share), 128), 4 * share)
            acc[...] += jnp.dot(xw[:, cols], weight_rows(unit * 4, 4), preferred_element_type=jnp.float32)

    def move_copy(k, quarter_at, device):
        ref = mbuf.at[quarter_at]
        cols = pl.ds(pl.multiple_of(y * quarter, HD), quarter)
        src = x_ref.at[pl.ds(CAP, MOVE), cols] if k == 0 else ref
        return pltpu.make_async_remote_copy(
            src_ref=src, dst_ref=ref, send_sem=ms.at[k], recv_sem=mr.at[k], device_id=device, device_id_type=MESH
        )

    def move_send(k):
        return move_copy(k, y, cross if k == 0 else (dp, ((y + k) % NY) * 2 + xh))

    def move_recv(k):
        return move_copy(k, (y - k + NY) % NY, cross)

    def swap(k, src, dst, device):
        return pltpu.make_async_remote_copy(
            src_ref=src, dst_ref=dst, send_sem=ps.at[k], recv_sem=pr.at[k], device_id=device, device_id_type=MESH
        )

    def with_sib(k, src, dst):
        return pltpu.make_async_remote_copy(
            src_ref=src, dst_ref=dst, send_sem=bs.at[k], recv_sem=br.at[k], device_id=sib, device_id_type=MESH
        )

    pair, lone = pl.ds(0, 2), pl.ds(2, 1)
    moved, tail = pl.ds(CAP, MOVE), pl.ds(BASE, MOVE)
    grads_swaps = (
        swap(0, gs.at[pair, moved], gm.at[pair], x_dev),
        swap(1, gs.at[lone, moved], gm.at[lone], cross),
    )
    att_swaps = (
        swap(2, attw.at[pair, tail], am.at[pair], x_dev),
        swap(3, attw.at[lone, tail], am.at[lone], cross),
    )
    out_swap = swap(4, outw, om, x_dev)
    weight_sib = with_sib(0, wrem, wbuf.at[b_own, 2])
    grads_sib = with_sib(1, grem, gs.at[2])
    att_sib = with_sib(2, ats.at[2], arem)

    def head(k):
        return pl.ds(pl.multiple_of(k * HD, HD), HD)

    kept = (head(xh), head(xh + 1))
    spare = head(2 - 2 * xh)
    same = xl == 0
    own_rows = pltpu.make_async_copy(x_ref.at[pl.ds(0, CAP)], xw, lsem)

    own_rows.start()
    for i in range(3):
        wrem[i] = w_ref[i, :, spare]
    for j in range(2):
        for i in range(3):
            wbuf[b_own, j, i] = w_ref[i, :, kept[j]]

    @pl.when(same)
    def _():
        wbuf[b_own, 2] = wrem[...]

    grem[...] = g_ref[:, spare]
    for j in range(2):
        gs[j] = g_ref[:, kept[j]]

    @pl.when(same)
    def _():
        gs[2] = grem[...]

    acc[...] = jnp.zeros_like(acc)
    own_ids = column(ids_ref, dp)
    other_ids = column(ids_ref, dev(1 - xl, z, c)[0])
    own_live = own_ids[:, :1] >= 0.0
    taken = [
        jnp.where(own >= 0.0, own, other)
        for own, other in zip(units(own_ids, BASE), units(other_ids, CAP)[::-1], strict=True)
    ]
    work_ids = jnp.concatenate([own_ids[:BASE], *taken], axis=0)
    pl.semaphore_wait(barrier, len(everyone))

    @pl.when(xl == 1)
    def _():
        weight_sib.start()

    for p in (3, 0, 1):
        x_send(0, 0, p).start()
    for p in (1, 2):
        for d in range(2):
            z_send(d, 1, p).start()

    @pl.when(xl == 1)
    def _():
        grads_sib.start()
        weight_sib.wait_recv()

    x_send(0, 0, 2).start()
    for d in range(2):
        z_send(d, 1, 3).start()
    c_send(0, 0, 0).start()
    x_recv(0, 0, 3).wait_recv()
    for d in range(2):
        z_send(d, 1, 0).start()
    move_send(0).start()

    def fill():
        for k in range(1, NY):
            move_recv(k).wait_recv()
        own_rows.wait()
        for at in range(MOVE // UNIT):
            mask = own_live[BASE + at * UNIT : BASE + (at + 1) * UNIT]
            rows = pl.ds(BASE + at * UNIT, UNIT)
            back = pl.ds(MOVE - (at + 1) * UNIT, UNIT)
            for q in range(NY):
                cols = pl.ds(q * quarter, quarter)
                xw[rows, cols] = pick(mask, xw[rows, cols], mbuf[q, back, :])

    order = (1, 2, 3, 0)
    last = {1: 0, 2: 0, 3: 1, 0: 1}
    far = NZ // 2

    def pass_x(d, s):
        for p in range(3):
            x_recv(d, s, p).wait_recv()
        c_send(d, s, 1).start()

    def landed(ds, s):
        for d in ds:
            for k in range(2):
                c_recv(d, s, k).wait_recv()

    def step(s, carry):
        for p in order:
            for d in range(2):
                z_recv(d, s, p).wait_recv()
                if last[p] == d:
                    z_send(d, s + 1, p).start()
                else:
                    @pl.when(s < far - 1)
                    def _():
                        z_send(d, s + 1, p).start()
                if p >= 1:
                    x_send(d, s, p - 1).start()
        for d in range(2):
            c_send(d, s, 0).start()

        @pl.when(s == 1)
        def _():
            pass_x(0, 0)

        @pl.when(s == 2)
        def _():
            landed((0,), 0)
            move_recv(0).wait_recv()
            for k in range(1, NY):
                move_send(k).start()

            @pl.when(xl == 1)
            def _():
                grads_sib.wait_recv()

            for copy in grads_swaps:
                copy.start()

        @pl.when(s > 1)
        def _():
            for d in range(2):
                pass_x(d, s - 1)

        @pl.when(s > 2)
        def _():
            landed((0, 1), s - 2)

        @pl.when(s == FILL)
        def _():
            fill()

        @pl.when(s >= FILL)
        def _():
            multiply(2 * (s - FILL) + 1)

        @pl.when((s >= FILL) & (s < far - 1))
        def _():
            multiply(2 * (s - FILL) + 2)

        return carry

    lax.fori_loop(1, far, step, 0)
    for p in order:
        z_recv(last[p], far, p).wait_recv()
        if p >= 1:
            x_send(0, far, p - 1).start()
    c_send(0, far, 0).start()
    for d in range(2):
        pass_x(d, far - 1)
    landed((0, 1), far - 2)
    multiply(far - 2)
    pass_x(0, far)
    landed((0, 1), far - 1)
    multiply(far - 1)
    landed((0,), far)
    multiply(far)

    qkv[...] = acc[...].astype(jnp.bfloat16)
    row_ids = work_ids.T[:1]
    allowed = (work_ids[:, :1] == row_ids) & (row_ids >= 0.0)
    live = (work_ids[:, :1] >= 0.0).astype(jnp.float32)
    for copy in grads_swaps:
        copy.wait_recv()
    for j in range(heads):
        gw[j, pl.ds(0, BASE)] = gs[j, pl.ds(0, BASE)]
        for at in range(MOVE // UNIT):
            rows = pl.ds(BASE + at * UNIT, UNIT)
            mask = own_live[BASE + at * UNIT : BASE + (at + 1) * UNIT]
            gw[j, rows] = pick(mask, gs[j, rows], gm[j, pl.ds(MOVE - (at + 1) * UNIT, UNIT)])
    for h in range(heads):
        at = [slice(i * width + h * HD, i * width + (h + 1) * HD) for i in range(3)]
        attended, *grads = attend_head(
            qkv[:, at[0]], qkv[:, at[1]], qkv[:, at[2]], gw[h], allowed, live
        )
        attw[h] = attended
        for i in range(3):
            gbuf[:, at[i]] = grads[i]

    for copy in att_swaps:
        copy.start()

    blocks = wbuf.shape[0] // 8

    def dest(i):
        k = i // 2
        dy = jnp.where(k < 2, k + 2, 3 - k)
        return ((y + dy) % NY) * 2 + (xh + 1 - i % 2) % 2

    parts = (pl.ds(BASE, MOVE), pl.ds(0, BASE))

    def sums(i, b):
        return pltpu.make_async_remote_copy(
            src_ref=sbuf.at[i, parts[b]], dst_ref=rbuf.at[i, parts[b]], send_sem=ts.at[b, i], recv_sem=tr.at[b, i],
            device_id=(dp, dest(i)), device_id_type=MESH,
        )

    def backward(i, carry):
        rows = weight_rows(dest(i) * blocks, blocks)
        sbuf[i] = lax.dot_general(
            gbuf[...], rows, (((1,), (1,)), ((), ())), preferred_element_type=jnp.float32
        ).astype(jnp.bfloat16)

        @pl.when(i < 7)
        def _():
            sums(i, 0).start()

        return carry

    lax.fori_loop(0, 8, backward, 0)

    def rest(i, carry):
        sums(i, 1).start()
        return carry

    lax.fori_loop(0, 7, rest, 0)

    for p in range(4):
        x_send(0, 0, p).wait_send()
    for k in range(2):
        c_send(0, 0, k).wait_send()

    def drain(s, carry):
        for d in range(2):
            for p in range(4):
                z_send(d, s, p).wait_send()
            for p in range(3):
                x_send(d, s, p).wait_send()
            for k in range(2):
                c_send(d, s, k).wait_send()
        return carry

    lax.fori_loop(1, NZ // 2, drain, 0)
    for p in range(4):
        z_send(last[p], far, p).wait_send()
    for p in range(3):
        x_send(0, far, p).wait_send()
    for k in range(2):
        c_send(0, far, k).wait_send()

    for k in range(NY):
        move_send(k).wait_send()
    for copy in grads_swaps:
        copy.wait_send()

    def give(ref, work, received):
        for at in range(MOVE // UNIT):
            for first, rows, index in ((BASE, work, at), (CAP, received, MOVE // UNIT - 1 - at)):
                here = first + at * UNIT
                if rows is not None:
                    mask = own_live[here : here + UNIT]
                    ref[pl.ds(here, UNIT)] = pick(mask, rows[pl.ds(index * UNIT, UNIT)], None)

    for copy in att_swaps:
        copy.wait()
    for j in range(heads):
        ats[j, pl.ds(0, BASE)] = attw[j, pl.ds(0, BASE)]
        give(ats.at[j], attw.at[j, tail], am.at[j])

    @pl.when(xl == 1)
    def _():
        att_sib.start()
        weight_sib.wait_send()
        grads_sib.wait_send()

    for j in range(2):
        att_ref[:, kept[j]] = ats[j]

    @pl.when(same)
    def _():
        att_ref[:, spare] = ats[2]

    def added(b):
        total = sbuf[7, parts[b]].astype(jnp.float32)
        for i in range(7):
            sums(i, b).wait_recv()
            total += rbuf[i, parts[b]].astype(jnp.float32)
        return total.astype(jnp.bfloat16)

    outw[...] = added(0)
    out_swap.start()

    @pl.when(xl == 1)
    def _():
        att_sib.wait()
        att_ref[:, spare] = arem[...]

    give(out_ref, outw, None)
    out_ref[pl.ds(0, BASE)] = added(1)
    out_swap.wait()
    give(out_ref, None, om)
    for b in range(2):
        for i in range(7):
            sums(i, b).wait_send()


def local(patches, qkv_weight, out_grad, image_starts):
    rows, model = patches.shape
    share = qkv_weight.shape[0]
    columns = qkv_weight.shape[1] * qkv_weight.shape[2]
    n_dp = model // share
    heads = columns // (3 * HD)
    vmem = pl.BlockSpec(memory_space=pltpu.VMEM)
    bf = jnp.bfloat16
    dma = pltpu.SemaphoreType.DMA
    steps = NZ // 2 + 1
    return pl.pallas_call(
        kernel,
        out_shape=(
            jax.ShapeDtypeStruct(out_grad.shape, bf),
            jax.ShapeDtypeStruct((rows, model // 8), bf),
        ),
        in_specs=[pl.BlockSpec(memory_space=pl.ANY), vmem, vmem, vmem],
        out_specs=(vmem, vmem),
        scratch_shapes=[
            pltpu.VMEM((n_dp, heads, 3, share, HD), bf),
            pltpu.VMEM((CAP, columns), jnp.float32),
            pltpu.VMEM((CAP, columns), bf),
            pltpu.VMEM((CAP, columns), bf),
            pltpu.VMEM((8, CAP, model // 8), bf),
            pltpu.VMEM((7, CAP, model // 8), bf),
            pltpu.VMEM((CAP, model), bf),
            pltpu.VMEM((NY, MOVE, model // NY), bf),
            pltpu.VMEM((3, share, HD), bf),
            pltpu.VMEM((rows, HD), bf),
            pltpu.VMEM((heads, rows, HD), bf),
            pltpu.VMEM((heads, CAP, HD), bf),
            pltpu.VMEM((heads, MOVE, HD), bf),
            pltpu.VMEM((heads, CAP, HD), bf),
            pltpu.VMEM((heads, MOVE, HD), bf),
            pltpu.VMEM((heads, rows, HD), bf),
            pltpu.VMEM((rows, HD), bf),
            pltpu.VMEM((MOVE, model // 8), bf),
            pltpu.VMEM((MOVE, model // 8), bf),
            dma((2, steps, 4)),
            dma((2, steps, 4)),
            dma((2, steps, 4)),
            dma((2, steps, 4)),
            dma((2, steps, 2)),
            dma((2, steps, 2)),
            dma((2, 8)),
            dma((2, 8)),
            dma((NY,)),
            dma((NY,)),
            dma((5,)),
            dma((5,)),
            dma((3,)),
            dma((3,)),
            dma(()),
        ],
        compiler_params=pltpu.CompilerParams(
            collective_id=0, has_side_effects=True, vmem_limit_bytes=56 * 1024 * 1024
        ),
    )(patches, qkv_weight.transpose(1, 0, 2), out_grad, image_starts)


def solution(mesh):
    in_specs = (P("dp", None), P("dp", None, "tensor"), P("dp", "tensor"), P())
    out_specs = (P("dp", "tensor"), P("dp", "tensor"))
    return jax.shard_map(local, mesh=mesh, in_specs=in_specs, out_specs=out_specs, check_vma=False)
```

```python
import functools

import jax
import jax.numpy as jnp
from jax import lax
from jax.experimental import pallas as pl
from jax.experimental.pallas import tpu as pltpu
from jax.sharding import PartitionSpec as P

HD = 128
NZ = 16
NY = 4
UNIT = 16
CAP = 160
MOVE = 64
BASE = CAP - MOVE
EARLY = 32
FILL = 5
MESH = pl.DeviceIdType.MESH


def attend_head(query, key, value, grad_out, allowed, live):
    score_scale = HD ** (-0.5)
    nt = (((1,), (1,)), ((), ()))
    tn = (((0,), (0,)), ((), ()))
    scores = lax.dot_general(query, key, nt, preferred_element_type=jnp.float32) * score_scale
    logits = jnp.where(allowed, scores, -1e30)
    top_score = jnp.max(logits, axis=-1, keepdims=True)
    expo = jnp.exp(logits - top_score)
    probs = expo / jnp.sum(expo, axis=-1, keepdims=True) * live
    low = probs.astype(jnp.bfloat16)
    attended = jnp.dot(low, value, preferred_element_type=jnp.float32).astype(jnp.bfloat16)
    grad_probs = lax.dot_general(grad_out, value, nt, preferred_element_type=jnp.float32)
    grad_value = lax.dot_general(low, grad_out, tn, preferred_element_type=jnp.float32).astype(jnp.bfloat16)
    row_delta = jnp.sum(probs * grad_probs, axis=-1, keepdims=True)
    grad_scores = (probs * (grad_probs - row_delta) * score_scale).astype(jnp.bfloat16)
    grad_query = jnp.dot(grad_scores, key, preferred_element_type=jnp.float32).astype(jnp.bfloat16)
    grad_key = lax.dot_general(grad_scores, query, tn, preferred_element_type=jnp.float32).astype(jnp.bfloat16)
    return attended, grad_query, grad_key, grad_value


def column(ids_ref, shard):
    row = ids_ref[pl.ds(shard, 1), :].astype(jnp.float32)
    return jnp.broadcast_to(row, (HD, row.shape[1])).T


def units(rows, first):
    return [rows[first + at : first + at + UNIT] for at in range(0, MOVE, UNIT)]


def pick(mask, there, other):
    kept = jnp.where(mask, there.astype(jnp.float32), other.astype(jnp.float32) if other is not None else 0.0)
    return kept.astype(there.dtype)


def kernel(
    x_ref, w_ref, g_ref, ids_ref, att_ref, out_ref,
    wbuf, acc, qkv, gbuf, sbuf, rbuf, xw, mbuf, wrem, grem, gs, gw, gm, attw, am, ats, arem, outw, om,
    zs, zr, xs, xr, cs, cr, ts, tr, ms, mr, ps, pr, bs, br, lsem,
):
    dp, t = lax.axis_index("dp"), lax.axis_index("tensor")
    xl, z, c = dp // (2 * NZ), (dp // 2) % NZ, dp % 2
    y, xh = t // 2, t % 2
    share, width = w_ref.shape[1:]
    b_own = dp
    quarter = xw.shape[1] // NY
    heads = width // HD

    def dev(xl_, z_, c_):
        return (xl_ * (2 * NZ) + z_ * 2 + c_, t)

    z_next = (dev(xl, (z + 1) % NZ, c), dev(xl, (z + NZ - 1) % NZ, c))
    x_dev = dev(1 - xl, z, c)
    c_dev = dev(xl, z, 1 - c)
    cross = (dev(1 - xl, z, c)[0], y * 2 + 1 - xh)
    sib = (dp, y * 2 + 1 - xh)
    peers = [(dp, ((y + j // 2) % NY) * 2 + (xh + j) % 2) for j in range(1, 8)]

    barrier = pltpu.get_barrier_semaphore()
    everyone = [*z_next, x_dev, c_dev, cross, *peers]
    for other in everyone:
        pl.semaphore_signal(barrier, inc=1, device_id=other, device_id_type=MESH)

    def origin(d, s):
        return (z - s + NZ) % NZ if d == 0 else (z + s) % NZ

    def block(xl_, z_, c_):
        return xl_ * (2 * NZ) + z_ * 2 + c_

    def x_ref_part(xl_, zo, p):
        at = block(xl_, zo, c)
        if p == 0:
            return wbuf.at[at, 0, :, pl.ds(EARLY, share - EARLY), :]
        return wbuf.at[at, 0, :, pl.ds(0, EARLY), :] if p == 3 else wbuf.at[at, p]

    def whole(xl_, z_, c_):
        return wbuf.at[block(xl_, z_, c_)]

    def z_ref(zo, p):
        return x_ref_part(1 - xl, zo, 3) if p == 0 else wbuf.at[block(xl, zo, c), p - 1]

    def remote(ref, send, recv, device):
        return pltpu.make_async_remote_copy(
            src_ref=ref, dst_ref=ref, send_sem=send, recv_sem=recv, device_id=device, device_id_type=MESH
        )

    def z_send(d, s, p):
        return remote(z_ref(origin(d, s - 1), p), zs.at[d, s, p], zr.at[d, s, p], z_next[d])

    def z_recv(d, s, p):
        return remote(z_ref(origin(d, s), p), zs.at[d, s, p], zr.at[d, s, p], z_next[d])

    def x_send(d, s, p):
        return remote(x_ref_part(xl, origin(d, s), p), xs.at[d, s, p], xr.at[d, s, p], cross if p == 2 else x_dev)

    def x_recv(d, s, p):
        return remote(x_ref_part(1 - xl, origin(d, s), p), xs.at[d, s, p], xr.at[d, s, p], cross if p == 2 else x_dev)

    def c_send(d, s, k):
        return remote(whole((xl + k) % 2, origin(d, s), c), cs.at[d, s, k], cr.at[d, s, k], c_dev)

    def c_recv(d, s, k):
        return remote(whole((xl + k) % 2, origin(d, s), 1 - c), cs.at[d, s, k], cr.at[d, s, k], c_dev)

    def weight_rows(first, count):
        return jnp.concatenate(
            [
                wbuf[pl.ds(first, count), j, i].reshape(count * share, HD)
                for i in range(3)
                for j in range(heads)
            ],
            axis=1,
        )

    def multiply(s):
        zc = jnp.where((z + s) % 2 == 1, (z + s) % NZ, (z - s + NZ) % NZ) // 2
        for half in range(2):
            unit = half * (NZ // 2) + zc
            cols = pl.ds(pl.multiple_of(unit * (4 * share), 128), 4 * share)
            acc[...] += jnp.dot(xw[:, cols], weight_rows(unit * 4, 4), preferred_element_type=jnp.float32)

    def move_copy(k, quarter_at, device):
        ref = mbuf.at[quarter_at]
        cols = pl.ds(pl.multiple_of(y * quarter, HD), quarter)
        src = x_ref.at[pl.ds(CAP, MOVE), cols] if k == 0 else ref
        return pltpu.make_async_remote_copy(
            src_ref=src, dst_ref=ref, send_sem=ms.at[k], recv_sem=mr.at[k], device_id=device, device_id_type=MESH
        )

    def move_send(k):
        return move_copy(k, y, cross if k == 0 else (dp, ((y + k) % NY) * 2 + xh))

    def move_recv(k):
        return move_copy(k, (y - k + NY) % NY, cross)

    def swap(k, src, dst, device):
        return pltpu.make_async_remote_copy(
            src_ref=src, dst_ref=dst, send_sem=ps.at[k], recv_sem=pr.at[k], device_id=device, device_id_type=MESH
        )

    def with_sib(k, src, dst):
        return pltpu.make_async_remote_copy(
            src_ref=src, dst_ref=dst, send_sem=bs.at[k], recv_sem=br.at[k], device_id=sib, device_id_type=MESH
        )

    pair, lone = pl.ds(0, 2), pl.ds(2, 1)
    moved, tail = pl.ds(CAP, MOVE), pl.ds(BASE, MOVE)
    grads_swaps = (
        swap(0, gs.at[pair, moved], gm.at[pair], x_dev),
        swap(1, gs.at[lone, moved], gm.at[lone], cross),
    )
    att_swaps = (
        swap(2, attw.at[pair, tail], am.at[pair], x_dev),
        swap(3, attw.at[lone, tail], am.at[lone], cross),
    )
    out_swap = swap(4, outw, om, x_dev)
    weight_sib = with_sib(0, wrem, wbuf.at[b_own, 2])
    grads_sib = with_sib(1, grem, gs.at[2])
    att_sib = with_sib(2, ats.at[2], arem)

    def head(k):
        return pl.ds(pl.multiple_of(k * HD, HD), HD)

    kept = (head(xh), head(xh + 1))
    spare = head(2 - 2 * xh)
    same = xl == 0
    own_rows = pltpu.make_async_copy(x_ref.at[pl.ds(0, CAP)], xw, lsem)

    own_rows.start()
    for i in range(3):
        wrem[i] = w_ref[i, :, spare]
    for j in range(2):
        for i in range(3):
            wbuf[b_own, j, i] = w_ref[i, :, kept[j]]

    @pl.when(same)
    def _():
        wbuf[b_own, 2] = wrem[...]

    grem[...] = g_ref[:, spare]
    for j in range(2):
        gs[j] = g_ref[:, kept[j]]

    @pl.when(same)
    def _():
        gs[2] = grem[...]

    acc[...] = jnp.zeros_like(acc)
    own_ids = column(ids_ref, dp)
    other_ids = column(ids_ref, dev(1 - xl, z, c)[0])
    own_live = own_ids[:, :1] >= 0.0
    taken = [
        jnp.where(own >= 0.0, own, other)
        for own, other in zip(units(own_ids, BASE), units(other_ids, CAP)[::-1], strict=True)
    ]
    work_ids = jnp.concatenate([own_ids[:BASE], *taken], axis=0)
    pl.semaphore_wait(barrier, len(everyone))

    @pl.when(xl == 1)
    def _():
        weight_sib.start()

    for p in (3, 0, 1):
        x_send(0, 0, p).start()
    for p in (1, 2):
        for d in range(2):
            z_send(d, 1, p).start()

    @pl.when(xl == 1)
    def _():
        grads_sib.start()
        weight_sib.wait_recv()

    x_send(0, 0, 2).start()
    for d in range(2):
        z_send(d, 1, 3).start()
    c_send(0, 0, 0).start()
    x_recv(0, 0, 3).wait_recv()
    for d in range(2):
        z_send(d, 1, 0).start()
    move_send(0).start()

    def fill():
        for k in range(1, NY):
            move_recv(k).wait_recv()
        own_rows.wait()
        for at in range(MOVE // UNIT):
            mask = own_live[BASE + at * UNIT : BASE + (at + 1) * UNIT]
            rows = pl.ds(BASE + at * UNIT, UNIT)
            back = pl.ds(MOVE - (at + 1) * UNIT, UNIT)
            for q in range(NY):
                cols = pl.ds(q * quarter, quarter)
                xw[rows, cols] = pick(mask, xw[rows, cols], mbuf[q, back, :])

    order = (1, 2, 3, 0)
    last = {1: 0, 2: 0, 3: 1, 0: 1}
    far = NZ // 2

    def pass_x(d, s):
        for p in range(3):
            x_recv(d, s, p).wait_recv()
        c_send(d, s, 1).start()

    def landed(ds, s):
        for d in ds:
            for k in range(2):
                c_recv(d, s, k).wait_recv()

    def step(s, carry):
        for p in order:
            for d in range(2):
                z_recv(d, s, p).wait_recv()
                if last[p] == d:
                    z_send(d, s + 1, p).start()
                else:
                    @pl.when(s < far - 1)
                    def _():
                        z_send(d, s + 1, p).start()
                if p >= 1:
                    x_send(d, s, p - 1).start()
        for d in range(2):
            c_send(d, s, 0).start()

        @pl.when(s == 1)
        def _():
            pass_x(0, 0)

        @pl.when(s == 2)
        def _():
            landed((0,), 0)
            move_recv(0).wait_recv()
            for k in range(1, NY):
                move_send(k).start()

            @pl.when(xl == 1)
            def _():
                grads_sib.wait_recv()

            for copy in grads_swaps:
                copy.start()

        @pl.when(s > 1)
        def _():
            for d in range(2):
                pass_x(d, s - 1)

        @pl.when(s > 2)
        def _():
            landed((0, 1), s - 2)

        @pl.when(s == FILL)
        def _():
            fill()

        @pl.when(s >= FILL)
        def _():
            multiply(2 * (s - FILL) + 1)

        @pl.when((s >= FILL) & (s < far - 1))
        def _():
            multiply(2 * (s - FILL) + 2)

        return carry

    lax.fori_loop(1, far, step, 0)
    for p in order:
        z_recv(last[p], far, p).wait_recv()
        if p >= 1:
            x_send(0, far, p - 1).start()
    c_send(0, far, 0).start()
    for d in range(2):
        pass_x(d, far - 1)
    landed((0, 1), far - 2)
    multiply(far - 2)
    pass_x(0, far)
    landed((0, 1), far - 1)
    multiply(far - 1)
    landed((0,), far)
    multiply(far)

    qkv[...] = acc[...].astype(jnp.bfloat16)
    row_ids = work_ids.T[:1]
    allowed = (work_ids[:, :1] == row_ids) & (row_ids >= 0.0)
    live = (work_ids[:, :1] >= 0.0).astype(jnp.float32)
    for copy in grads_swaps:
        copy.wait_recv()
    for j in range(heads):
        gw[j, pl.ds(0, BASE)] = gs[j, pl.ds(0, BASE)]
        for at in range(MOVE // UNIT):
            rows = pl.ds(BASE + at * UNIT, UNIT)
            mask = own_live[BASE + at * UNIT : BASE + (at + 1) * UNIT]
            gw[j, rows] = pick(mask, gs[j, rows], gm[j, pl.ds(MOVE - (at + 1) * UNIT, UNIT)])
    for h in range(heads):
        at = [slice(i * width + h * HD, i * width + (h + 1) * HD) for i in range(3)]
        attended, *grads = attend_head(
            qkv[:, at[0]], qkv[:, at[1]], qkv[:, at[2]], gw[h], allowed, live
        )
        attw[h] = attended
        for i in range(3):
            gbuf[:, at[i]] = grads[i]

    for copy in att_swaps:
        copy.start()

    blocks = wbuf.shape[0] // 8

    def dest(i):
        k = i // 2
        dy = jnp.where(k < 2, k + 2, 3 - k)
        return ((y + dy) % NY) * 2 + (xh + 1 - i % 2) % 2

    parts = (pl.ds(BASE, MOVE), pl.ds(0, BASE))

    def sums(i, b):
        return pltpu.make_async_remote_copy(
            src_ref=sbuf.at[i, parts[b]], dst_ref=rbuf.at[i, parts[b]], send_sem=ts.at[b, i], recv_sem=tr.at[b, i],
            device_id=(dp, dest(i)), device_id_type=MESH,
        )

    def backward(i, carry):
        rows = weight_rows(dest(i) * blocks, blocks)
        sbuf[i] = lax.dot_general(
            gbuf[...], rows, (((1,), (1,)), ((), ())), preferred_element_type=jnp.float32
        ).astype(jnp.bfloat16)

        @pl.when(i < 7)
        def _():
            sums(i, 0).start()

        return carry

    lax.fori_loop(0, 8, backward, 0)

    def rest(i, carry):
        sums(i, 1).start()
        return carry

    lax.fori_loop(0, 7, rest, 0)

    for p in range(4):
        x_send(0, 0, p).wait_send()
    for k in range(2):
        c_send(0, 0, k).wait_send()

    def drain(s, carry):
        for d in range(2):
            for p in range(4):
                z_send(d, s, p).wait_send()
            for p in range(3):
                x_send(d, s, p).wait_send()
            for k in range(2):
                c_send(d, s, k).wait_send()
        return carry

    lax.fori_loop(1, NZ // 2, drain, 0)
    for p in range(4):
        z_send(last[p], far, p).wait_send()
    for p in range(3):
        x_send(0, far, p).wait_send()
    for k in range(2):
        c_send(0, far, k).wait_send()

    for k in range(NY):
        move_send(k).wait_send()
    for copy in grads_swaps:
        copy.wait_send()

    def give(ref, work, received):
        for at in range(MOVE // UNIT):
            for first, rows, index in ((BASE, work, at), (CAP, received, MOVE // UNIT - 1 - at)):
                here = first + at * UNIT
                if rows is not None:
                    mask = own_live[here : here + UNIT]
                    ref[pl.ds(here, UNIT)] = pick(mask, rows[pl.ds(index * UNIT, UNIT)], None)

    for copy in att_swaps:
        copy.wait()
    for j in range(heads):
        ats[j, pl.ds(0, BASE)] = attw[j, pl.ds(0, BASE)]
        give(ats.at[j], attw.at[j, tail], am.at[j])

    @pl.when(xl == 1)
    def _():
        att_sib.start()
        weight_sib.wait_send()
        grads_sib.wait_send()

    for j in range(2):
        att_ref[:, kept[j]] = ats[j]

    @pl.when(same)
    def _():
        att_ref[:, spare] = ats[2]

    def added(b):
        total = sbuf[7, parts[b]].astype(jnp.float32)
        for i in range(7):
            sums(i, b).wait_recv()
            total += rbuf[i, parts[b]].astype(jnp.float32)
        return total.astype(jnp.bfloat16)

    outw[...] = added(0)
    out_swap.start()

    @pl.when(xl == 1)
    def _():
        att_sib.wait()
        att_ref[:, spare] = arem[...]

    give(out_ref, outw, None)
    out_ref[pl.ds(0, BASE)] = added(1)
    out_swap.wait()
    give(out_ref, None, om)
    for b in range(2):
        for i in range(7):
            sums(i, b).wait_send()


def deliver_kernel(a_ref, b_ref, c_ref, d_ref):
    c_ref[...] = a_ref[...]
    d_ref[...] = b_ref[...]


def deliver(*arrays):
    vmem = pl.BlockSpec(memory_space=pltpu.VMEM)
    return pl.pallas_call(
        deliver_kernel,
        out_shape=tuple(jax.ShapeDtypeStruct(a.shape, a.dtype) for a in arrays),
        in_specs=[vmem] * 2,
        out_specs=(vmem, vmem),
    )(*arrays)


def local(patches, qkv_weight, out_grad, image_starts):
    rows, model = patches.shape
    share = qkv_weight.shape[0]
    columns = qkv_weight.shape[1] * qkv_weight.shape[2]
    n_dp = model // share
    heads = columns // (3 * HD)
    vmem = pl.BlockSpec(memory_space=pltpu.VMEM)
    bf = jnp.bfloat16
    dma = pltpu.SemaphoreType.DMA
    steps = NZ // 2 + 1
    attended, patch_grad = pl.pallas_call(
        kernel,
        out_shape=(
            jax.ShapeDtypeStruct(out_grad.shape, bf),
            jax.ShapeDtypeStruct((rows, model // 8), bf),
        ),
        in_specs=[pl.BlockSpec(memory_space=pl.ANY), vmem, vmem, vmem],
        out_specs=(vmem, vmem),
        scratch_shapes=[
            pltpu.VMEM((n_dp, heads, 3, share, HD), bf),
            pltpu.VMEM((CAP, columns), jnp.float32),
            pltpu.VMEM((CAP, columns), bf),
            pltpu.VMEM((CAP, columns), bf),
            pltpu.VMEM((8, CAP, model // 8), bf),
            pltpu.VMEM((7, CAP, model // 8), bf),
            pltpu.VMEM((CAP, model), bf),
            pltpu.VMEM((NY, MOVE, model // NY), bf),
            pltpu.VMEM((3, share, HD), bf),
            pltpu.VMEM((rows, HD), bf),
            pltpu.VMEM((heads, rows, HD), bf),
            pltpu.VMEM((heads, CAP, HD), bf),
            pltpu.VMEM((heads, MOVE, HD), bf),
            pltpu.VMEM((heads, CAP, HD), bf),
            pltpu.VMEM((heads, MOVE, HD), bf),
            pltpu.VMEM((heads, rows, HD), bf),
            pltpu.VMEM((rows, HD), bf),
            pltpu.VMEM((MOVE, model // 8), bf),
            pltpu.VMEM((MOVE, model // 8), bf),
            dma((2, steps, 4)),
            dma((2, steps, 4)),
            dma((2, steps, 4)),
            dma((2, steps, 4)),
            dma((2, steps, 2)),
            dma((2, steps, 2)),
            dma((2, 8)),
            dma((2, 8)),
            dma((NY,)),
            dma((NY,)),
            dma((5,)),
            dma((5,)),
            dma((3,)),
            dma((3,)),
            dma(()),
        ],
        compiler_params=pltpu.CompilerParams(
            collective_id=0, has_side_effects=True, vmem_limit_bytes=56 * 1024 * 1024
        ),
    )(patches, qkv_weight.transpose(1, 0, 2), out_grad, image_starts)
    return deliver(attended, patch_grad)


def solution(mesh):
    in_specs = (P("dp", None), P("dp", None, "tensor"), P("dp", "tensor"), P())
    out_specs = (P("dp", "tensor"), P("dp", "tensor"))
    return jax.shard_map(local, mesh=mesh, in_specs=in_specs, out_specs=out_specs, check_vma=False)
```

```python
import functools

import jax
import jax.numpy as jnp
from jax import lax
from jax.experimental import pallas as pl
from jax.experimental.pallas import tpu as pltpu
from jax.sharding import PartitionSpec as P

HD = 128
NZ = 16
NY = 4
UNIT = 16
CAP = 160
MOVE = 64
BASE = CAP - MOVE
EARLY = 32
FILL = 5
MESH = pl.DeviceIdType.MESH


def attend_head(query, key, value, grad_out, allowed, live):
    score_scale = HD ** (-0.5)
    nt = (((1,), (1,)), ((), ()))
    tn = (((0,), (0,)), ((), ()))
    scores = lax.dot_general(query, key, nt, preferred_element_type=jnp.float32) * score_scale
    logits = jnp.where(allowed, scores, -1e30)
    top_score = jnp.max(logits, axis=-1, keepdims=True)
    expo = jnp.exp(logits - top_score)
    probs = expo / jnp.sum(expo, axis=-1, keepdims=True) * live
    low = probs.astype(jnp.bfloat16)
    attended = jnp.dot(low, value, preferred_element_type=jnp.float32).astype(jnp.bfloat16)
    grad_probs = lax.dot_general(grad_out, value, nt, preferred_element_type=jnp.float32)
    grad_value = lax.dot_general(low, grad_out, tn, preferred_element_type=jnp.float32).astype(jnp.bfloat16)
    row_delta = jnp.sum(probs * grad_probs, axis=-1, keepdims=True)
    grad_scores = (probs * (grad_probs - row_delta) * score_scale).astype(jnp.bfloat16)
    grad_query = jnp.dot(grad_scores, key, preferred_element_type=jnp.float32).astype(jnp.bfloat16)
    grad_key = lax.dot_general(grad_scores, query, tn, preferred_element_type=jnp.float32).astype(jnp.bfloat16)
    return attended, grad_query, grad_key, grad_value


def column(ids_ref, shard):
    row = ids_ref[pl.ds(shard, 1), :].astype(jnp.float32)
    return jnp.broadcast_to(row, (HD, row.shape[1])).T


def units(rows, first):
    return [rows[first + at : first + at + UNIT] for at in range(0, MOVE, UNIT)]


def pick(mask, there, other):
    kept = jnp.where(mask, there.astype(jnp.float32), other.astype(jnp.float32) if other is not None else 0.0)
    return kept.astype(there.dtype)


def kernel(
    x_ref, w_ref, g_ref, ids_ref, att_ref, out_ref,
    wbuf, acc, qkv, gbuf, sbuf, rbuf, xw, mbuf, wrem, grem, gs, gw, gm, attw, am, ats, arem, outw, om,
    zs, zr, xs, xr, cs, cr, ts, tr, ms, mr, ps, pr, bs, br, lsem,
):
    dp, t = lax.axis_index("dp"), lax.axis_index("tensor")
    xl, z, c = dp // (2 * NZ), (dp // 2) % NZ, dp % 2
    y, xh = t // 2, t % 2
    share, width = w_ref.shape[1:]
    b_own = dp
    quarter = xw.shape[1] // NY
    heads = width // HD

    def dev(xl_, z_, c_):
        return (xl_ * (2 * NZ) + z_ * 2 + c_, t)

    z_next = (dev(xl, (z + 1) % NZ, c), dev(xl, (z + NZ - 1) % NZ, c))
    x_dev = dev(1 - xl, z, c)
    c_dev = dev(xl, z, 1 - c)
    cross = (dev(1 - xl, z, c)[0], y * 2 + 1 - xh)
    sib = (dp, y * 2 + 1 - xh)
    peers = [(dp, ((y + j // 2) % NY) * 2 + (xh + j) % 2) for j in range(1, 8)]

    barrier = pltpu.get_barrier_semaphore()
    everyone = [*z_next, x_dev, c_dev, cross, *peers]
    for other in everyone:
        pl.semaphore_signal(barrier, inc=1, device_id=other, device_id_type=MESH)

    def origin(d, s):
        return (z - s + NZ) % NZ if d == 0 else (z + s) % NZ

    def block(xl_, z_, c_):
        return xl_ * (2 * NZ) + z_ * 2 + c_

    def x_ref_part(xl_, zo, p):
        at = block(xl_, zo, c)
        if p == 0:
            return wbuf.at[at, 0, :, pl.ds(EARLY, share - EARLY), :]
        return wbuf.at[at, 0, :, pl.ds(0, EARLY), :] if p == 3 else wbuf.at[at, p]

    def whole(xl_, z_, c_):
        return wbuf.at[block(xl_, z_, c_)]

    def z_ref(zo, p):
        return x_ref_part(1 - xl, zo, 3) if p == 0 else wbuf.at[block(xl, zo, c), p - 1]

    def remote(ref, send, recv, device):
        return pltpu.make_async_remote_copy(
            src_ref=ref, dst_ref=ref, send_sem=send, recv_sem=recv, device_id=device, device_id_type=MESH
        )

    def z_send(d, s, p):
        return remote(z_ref(origin(d, s - 1), p), zs.at[d, s, p], zr.at[d, s, p], z_next[d])

    def z_recv(d, s, p):
        return remote(z_ref(origin(d, s), p), zs.at[d, s, p], zr.at[d, s, p], z_next[d])

    def x_send(d, s, p):
        return remote(x_ref_part(xl, origin(d, s), p), xs.at[d, s, p], xr.at[d, s, p], cross if p == 2 else x_dev)

    def x_recv(d, s, p):
        return remote(x_ref_part(1 - xl, origin(d, s), p), xs.at[d, s, p], xr.at[d, s, p], cross if p == 2 else x_dev)

    def c_send(d, s, k):
        return remote(whole((xl + k) % 2, origin(d, s), c), cs.at[d, s, k], cr.at[d, s, k], c_dev)

    def c_recv(d, s, k):
        return remote(whole((xl + k) % 2, origin(d, s), 1 - c), cs.at[d, s, k], cr.at[d, s, k], c_dev)

    def weight_rows(first, count):
        return jnp.concatenate(
            [
                wbuf[pl.ds(first, count), j, i].reshape(count * share, HD)
                for i in range(3)
                for j in range(heads)
            ],
            axis=1,
        )

    def multiply(s):
        zc = jnp.where((z + s) % 2 == 1, (z + s) % NZ, (z - s + NZ) % NZ) // 2
        for half in range(2):
            unit = half * (NZ // 2) + zc
            cols = pl.ds(pl.multiple_of(unit * (4 * share), 128), 4 * share)
            acc[...] += jnp.dot(xw[:, cols], weight_rows(unit * 4, 4), preferred_element_type=jnp.float32)

    def move_copy(k, quarter_at, device):
        ref = mbuf.at[quarter_at]
        cols = pl.ds(pl.multiple_of(y * quarter, HD), quarter)
        src = x_ref.at[pl.ds(CAP, MOVE), cols] if k == 0 else ref
        return pltpu.make_async_remote_copy(
            src_ref=src, dst_ref=ref, send_sem=ms.at[k], recv_sem=mr.at[k], device_id=device, device_id_type=MESH
        )

    def move_send(k):
        return move_copy(k, y, cross if k == 0 else (dp, ((y + k) % NY) * 2 + xh))

    def move_recv(k):
        return move_copy(k, (y - k + NY) % NY, cross)

    def swap(k, src, dst, device):
        return pltpu.make_async_remote_copy(
            src_ref=src, dst_ref=dst, send_sem=ps.at[k], recv_sem=pr.at[k], device_id=device, device_id_type=MESH
        )

    def with_sib(k, src, dst):
        return pltpu.make_async_remote_copy(
            src_ref=src, dst_ref=dst, send_sem=bs.at[k], recv_sem=br.at[k], device_id=sib, device_id_type=MESH
        )

    pair, lone = pl.ds(0, 2), pl.ds(2, 1)
    moved, tail = pl.ds(CAP, MOVE), pl.ds(BASE, MOVE)
    grads_swaps = (
        swap(0, gs.at[pair, moved], gm.at[pair], x_dev),
        swap(1, gs.at[lone, moved], gm.at[lone], cross),
    )
    att_swaps = (
        swap(2, attw.at[pair, tail], am.at[pair], x_dev),
        swap(3, attw.at[lone, tail], am.at[lone], cross),
    )
    out_swap = swap(4, outw, om, x_dev)
    weight_sib = with_sib(0, wrem, wbuf.at[b_own, 2])
    grads_sib = with_sib(1, grem, gs.at[2])
    att_sib = with_sib(2, ats.at[2], arem)

    def head(k):
        return pl.ds(pl.multiple_of(k * HD, HD), HD)

    kept = (head(xh), head(xh + 1))
    spare = head(2 - 2 * xh)
    same = xl == 0
    own_rows = pltpu.make_async_copy(x_ref.at[pl.ds(0, CAP)], xw, lsem)

    own_rows.start()
    for i in range(3):
        wrem[i] = w_ref[i, :, spare]
    for j in range(2):
        for i in range(3):
            wbuf[b_own, j, i] = w_ref[i, :, kept[j]]

    @pl.when(same)
    def _():
        wbuf[b_own, 2] = wrem[...]

    grem[...] = g_ref[:, spare]
    for j in range(2):
        gs[j] = g_ref[:, kept[j]]

    @pl.when(same)
    def _():
        gs[2] = grem[...]

    acc[...] = jnp.zeros_like(acc)
    own_ids = column(ids_ref, dp)
    other_ids = column(ids_ref, dev(1 - xl, z, c)[0])
    own_live = own_ids[:, :1] >= 0.0
    taken = [
        jnp.where(own >= 0.0, own, other)
        for own, other in zip(units(own_ids, BASE), units(other_ids, CAP)[::-1], strict=True)
    ]
    work_ids = jnp.concatenate([own_ids[:BASE], *taken], axis=0)
    pl.semaphore_wait(barrier, len(everyone))

    @pl.when(xl == 1)
    def _():
        weight_sib.start()

    for p in (3, 0, 1):
        x_send(0, 0, p).start()
    for p in (1, 2):
        for d in range(2):
            z_send(d, 1, p).start()

    @pl.when(xl == 1)
    def _():
        grads_sib.start()
        weight_sib.wait_recv()

    x_send(0, 0, 2).start()
    for d in range(2):
        z_send(d, 1, 3).start()
    c_send(0, 0, 0).start()
    x_recv(0, 0, 3).wait_recv()
    for d in range(2):
        z_send(d, 1, 0).start()
    move_send(0).start()

    def fill():
        for k in range(1, NY):
            move_recv(k).wait_recv()
        own_rows.wait()
        for at in range(MOVE // UNIT):
            mask = own_live[BASE + at * UNIT : BASE + (at + 1) * UNIT]
            rows = pl.ds(BASE + at * UNIT, UNIT)
            back = pl.ds(MOVE - (at + 1) * UNIT, UNIT)
            for q in range(NY):
                cols = pl.ds(q * quarter, quarter)
                xw[rows, cols] = pick(mask, xw[rows, cols], mbuf[q, back, :])

    order = (1, 2, 3, 0)
    last = {1: 0, 2: 1, 3: 1, 0: 0}
    far = NZ // 2

    def pass_x(d, s):
        for p in range(3):
            x_recv(d, s, p).wait_recv()
        c_send(d, s, 1).start()

    def landed(ds, s):
        for d in ds:
            for k in range(2):
                c_recv(d, s, k).wait_recv()

    def step(s, carry):
        for p in order:
            for d in range(2):
                z_recv(d, s, p).wait_recv()
                if last[p] == d:
                    z_send(d, s + 1, p).start()
                else:
                    @pl.when(s < far - 1)
                    def _():
                        z_send(d, s + 1, p).start()
                if p >= 1:
                    x_send(d, s, p - 1).start()
        for d in range(2):
            c_send(d, s, 0).start()

        @pl.when(s == 1)
        def _():
            pass_x(0, 0)

        @pl.when(s == 2)
        def _():
            landed((0,), 0)
            move_recv(0).wait_recv()
            for k in range(1, NY):
                move_send(k).start()

            @pl.when(xl == 1)
            def _():
                grads_sib.wait_recv()

            for copy in grads_swaps:
                copy.start()

        @pl.when(s > 1)
        def _():
            for d in range(2):
                pass_x(d, s - 1)

        @pl.when(s > 2)
        def _():
            landed((0, 1), s - 2)

        @pl.when(s == FILL)
        def _():
            fill()

        @pl.when(s >= FILL)
        def _():
            multiply(2 * (s - FILL) + 1)

        @pl.when((s >= FILL) & (s < far - 1))
        def _():
            multiply(2 * (s - FILL) + 2)

        return carry

    lax.fori_loop(1, far, step, 0)
    for p in order:
        z_recv(last[p], far, p).wait_recv()
        if p >= 1:
            x_send(0, far, p - 1).start()
    c_send(0, far, 0).start()
    for d in range(2):
        pass_x(d, far - 1)
    landed((0, 1), far - 2)
    multiply(far - 2)
    pass_x(0, far)
    landed((0, 1), far - 1)
    multiply(far - 1)
    landed((0,), far)
    multiply(far)

    qkv[...] = acc[...].astype(jnp.bfloat16)
    row_ids = work_ids.T[:1]
    allowed = (work_ids[:, :1] == row_ids) & (row_ids >= 0.0)
    live = (work_ids[:, :1] >= 0.0).astype(jnp.float32)
    for copy in grads_swaps:
        copy.wait_recv()
    for j in range(heads):
        gw[j, pl.ds(0, BASE)] = gs[j, pl.ds(0, BASE)]
        for at in range(MOVE // UNIT):
            rows = pl.ds(BASE + at * UNIT, UNIT)
            mask = own_live[BASE + at * UNIT : BASE + (at + 1) * UNIT]
            gw[j, rows] = pick(mask, gs[j, rows], gm[j, pl.ds(MOVE - (at + 1) * UNIT, UNIT)])
    for h in range(heads):
        at = [slice(i * width + h * HD, i * width + (h + 1) * HD) for i in range(3)]
        attended, *grads = attend_head(
            qkv[:, at[0]], qkv[:, at[1]], qkv[:, at[2]], gw[h], allowed, live
        )
        attw[h] = attended
        for i in range(3):
            gbuf[:, at[i]] = grads[i]

    for copy in att_swaps:
        copy.start()

    blocks = wbuf.shape[0] // 8

    def dest(i):
        k = i // 2
        dy = jnp.where(k < 2, 2 * k + 1, jnp.where(k == 2, 2, 0))
        return ((y + dy) % NY) * 2 + (xh + 1 - i % 2) % 2

    parts = (pl.ds(BASE, MOVE), pl.ds(0, BASE))

    def sums(i, b):
        return pltpu.make_async_remote_copy(
            src_ref=sbuf.at[i, parts[b]], dst_ref=rbuf.at[i, parts[b]], send_sem=ts.at[b, i], recv_sem=tr.at[b, i],
            device_id=(dp, dest(i)), device_id_type=MESH,
        )

    def backward(i, carry):
        rows = weight_rows(dest(i) * blocks, blocks)
        sbuf[i] = lax.dot_general(
            gbuf[...], rows, (((1,), (1,)), ((), ())), preferred_element_type=jnp.float32
        ).astype(jnp.bfloat16)

        @pl.when(i < 7)
        def _():
            sums(i, 0).start()

        return carry

    lax.fori_loop(0, 8, backward, 0)

    def rest(i, carry):
        sums(i, 1).start()
        return carry

    lax.fori_loop(0, 7, rest, 0)

    for p in range(4):
        x_send(0, 0, p).wait_send()
    for k in range(2):
        c_send(0, 0, k).wait_send()

    def drain(s, carry):
        for d in range(2):
            for p in range(4):
                z_send(d, s, p).wait_send()
            for p in range(3):
                x_send(d, s, p).wait_send()
            for k in range(2):
                c_send(d, s, k).wait_send()
        return carry

    lax.fori_loop(1, NZ // 2, drain, 0)
    for p in range(4):
        z_send(last[p], far, p).wait_send()
    for p in range(3):
        x_send(0, far, p).wait_send()
    for k in range(2):
        c_send(0, far, k).wait_send()

    for k in range(NY):
        move_send(k).wait_send()
    for copy in grads_swaps:
        copy.wait_send()

    def give(ref, work, received):
        for at in range(MOVE // UNIT):
            for first, rows, index in ((BASE, work, at), (CAP, received, MOVE // UNIT - 1 - at)):
                here = first + at * UNIT
                if rows is not None:
                    mask = own_live[here : here + UNIT]
                    ref[pl.ds(here, UNIT)] = pick(mask, rows[pl.ds(index * UNIT, UNIT)], None)

    for copy in att_swaps:
        copy.wait()
    for j in range(heads):
        ats[j, pl.ds(0, BASE)] = attw[j, pl.ds(0, BASE)]
        give(ats.at[j], attw.at[j, tail], am.at[j])

    @pl.when(xl == 1)
    def _():
        att_sib.start()
        weight_sib.wait_send()
        grads_sib.wait_send()

    for j in range(2):
        att_ref[:, kept[j]] = ats[j]

    @pl.when(same)
    def _():
        att_ref[:, spare] = ats[2]

    def added(b):
        total = sbuf[7, parts[b]].astype(jnp.float32)
        for i in range(7):
            sums(i, b).wait_recv()
            total += rbuf[i, parts[b]].astype(jnp.float32)
        return total.astype(jnp.bfloat16)

    outw[...] = added(0)
    out_swap.start()

    @pl.when(xl == 1)
    def _():
        att_sib.wait()
        att_ref[:, spare] = arem[...]

    give(out_ref, outw, None)
    out_ref[pl.ds(0, BASE)] = added(1)
    out_swap.wait()
    give(out_ref, None, om)
    for b in range(2):
        for i in range(7):
            sums(i, b).wait_send()


def deliver_kernel(a_ref, b_ref, c_ref, d_ref):
    c_ref[...] = a_ref[...]
    d_ref[...] = b_ref[...]


def deliver(*arrays):
    vmem = pl.BlockSpec(memory_space=pltpu.VMEM)
    return pl.pallas_call(
        deliver_kernel,
        out_shape=tuple(jax.ShapeDtypeStruct(a.shape, a.dtype) for a in arrays),
        in_specs=[vmem] * 2,
        out_specs=(vmem, vmem),
    )(*arrays)


def local(patches, qkv_weight, out_grad, image_starts):
    rows, model = patches.shape
    share = qkv_weight.shape[0]
    columns = qkv_weight.shape[1] * qkv_weight.shape[2]
    n_dp = model // share
    heads = columns // (3 * HD)
    vmem = pl.BlockSpec(memory_space=pltpu.VMEM)
    bf = jnp.bfloat16
    dma = pltpu.SemaphoreType.DMA
    steps = NZ // 2 + 1
    attended, patch_grad = pl.pallas_call(
        kernel,
        out_shape=(
            jax.ShapeDtypeStruct(out_grad.shape, bf),
            jax.ShapeDtypeStruct((rows, model // 8), bf),
        ),
        in_specs=[pl.BlockSpec(memory_space=pl.ANY), vmem, vmem, vmem],
        out_specs=(vmem, vmem),
        scratch_shapes=[
            pltpu.VMEM((n_dp, heads, 3, share, HD), bf),
            pltpu.VMEM((CAP, columns), jnp.float32),
            pltpu.VMEM((CAP, columns), bf),
            pltpu.VMEM((CAP, columns), bf),
            pltpu.VMEM((8, CAP, model // 8), bf),
            pltpu.VMEM((7, CAP, model // 8), bf),
            pltpu.VMEM((CAP, model), bf),
            pltpu.VMEM((NY, MOVE, model // NY), bf),
            pltpu.VMEM((3, share, HD), bf),
            pltpu.VMEM((rows, HD), bf),
            pltpu.VMEM((heads, rows, HD), bf),
            pltpu.VMEM((heads, CAP, HD), bf),
            pltpu.VMEM((heads, MOVE, HD), bf),
            pltpu.VMEM((heads, CAP, HD), bf),
            pltpu.VMEM((heads, MOVE, HD), bf),
            pltpu.VMEM((heads, rows, HD), bf),
            pltpu.VMEM((rows, HD), bf),
            pltpu.VMEM((MOVE, model // 8), bf),
            pltpu.VMEM((MOVE, model // 8), bf),
            dma((2, steps, 4)),
            dma((2, steps, 4)),
            dma((2, steps, 4)),
            dma((2, steps, 4)),
            dma((2, steps, 2)),
            dma((2, steps, 2)),
            dma((2, 8)),
            dma((2, 8)),
            dma((NY,)),
            dma((NY,)),
            dma((5,)),
            dma((5,)),
            dma((3,)),
            dma((3,)),
            dma(()),
        ],
        compiler_params=pltpu.CompilerParams(
            collective_id=0, has_side_effects=True, vmem_limit_bytes=56 * 1024 * 1024
        ),
    )(patches, qkv_weight.transpose(1, 0, 2), out_grad, image_starts)
    return deliver(attended, patch_grad)


def solution(mesh):
    in_specs = (P("dp", None), P("dp", None, "tensor"), P("dp", "tensor"), P())
    out_specs = (P("dp", "tensor"), P("dp", "tensor"))
    return jax.shard_map(local, mesh=mesh, in_specs=in_specs, out_specs=out_specs, check_vma=False)
```

```python
import functools

import jax
import jax.numpy as jnp
from jax import lax
from jax.experimental import pallas as pl
from jax.experimental.pallas import tpu as pltpu
from jax.sharding import PartitionSpec as P

HD = 128
NZ = 16
NY = 4
UNIT = 16
CAP = 160
MOVE = 64
BASE = CAP - MOVE
EARLY = 32
FILL = 5
MESH = pl.DeviceIdType.MESH


def attend_head(query, key, value, grad_out, allowed, live):
    score_scale = HD ** (-0.5)
    nt = (((1,), (1,)), ((), ()))
    tn = (((0,), (0,)), ((), ()))
    scores = lax.dot_general(query, key, nt, preferred_element_type=jnp.float32) * score_scale
    logits = jnp.where(allowed, scores, -1e30)
    top_score = jnp.max(logits, axis=-1, keepdims=True)
    expo = jnp.exp(logits - top_score)
    probs = expo / jnp.sum(expo, axis=-1, keepdims=True) * live
    low = probs.astype(jnp.bfloat16)
    attended = jnp.dot(low, value, preferred_element_type=jnp.float32).astype(jnp.bfloat16)
    grad_probs = lax.dot_general(grad_out, value, nt, preferred_element_type=jnp.float32)
    grad_value = lax.dot_general(low, grad_out, tn, preferred_element_type=jnp.float32).astype(jnp.bfloat16)
    row_delta = jnp.sum(probs * grad_probs, axis=-1, keepdims=True)
    grad_scores = (probs * (grad_probs - row_delta) * score_scale).astype(jnp.bfloat16)
    grad_query = jnp.dot(grad_scores, key, preferred_element_type=jnp.float32).astype(jnp.bfloat16)
    grad_key = lax.dot_general(grad_scores, query, tn, preferred_element_type=jnp.float32).astype(jnp.bfloat16)
    return attended, grad_query, grad_key, grad_value


def column(ids_ref, shard):
    row = ids_ref[pl.ds(shard, 1), :].astype(jnp.float32)
    return jnp.broadcast_to(row, (HD, row.shape[1])).T


def units(rows, first):
    return [rows[first + at : first + at + UNIT] for at in range(0, MOVE, UNIT)]


def pick(mask, there, other):
    kept = jnp.where(mask, there.astype(jnp.float32), other.astype(jnp.float32) if other is not None else 0.0)
    return kept.astype(there.dtype)


def kernel(
    x_ref, w_ref, g_ref, ids_ref, att_ref, out_ref,
    wbuf, acc, qkv, gbuf, sbuf, rbuf, xw, mbuf, wrem, grem, gs, gw, gm, attw, am, ats, arem, outw, om,
    zs, zr, xs, xr, cs, cr, ts, tr, ms, mr, ps, pr, bs, br, lsem,
):
    dp, t = lax.axis_index("dp"), lax.axis_index("tensor")
    xl, z, c = dp // (2 * NZ), (dp // 2) % NZ, dp % 2
    y, xh = t // 2, t % 2
    share, width = w_ref.shape[1:]
    b_own = dp
    quarter = xw.shape[1] // NY
    heads = width // HD

    def dev(xl_, z_, c_):
        return (xl_ * (2 * NZ) + z_ * 2 + c_, t)

    z_next = (dev(xl, (z + 1) % NZ, c), dev(xl, (z + NZ - 1) % NZ, c))
    x_dev = dev(1 - xl, z, c)
    c_dev = dev(xl, z, 1 - c)
    cross = (dev(1 - xl, z, c)[0], y * 2 + 1 - xh)
    sib = (dp, y * 2 + 1 - xh)
    peers = [(dp, ((y + j // 2) % NY) * 2 + (xh + j) % 2) for j in range(1, 8)]

    barrier = pltpu.get_barrier_semaphore()
    everyone = [*z_next, x_dev, c_dev, cross, *peers]
    for other in everyone:
        pl.semaphore_signal(barrier, inc=1, device_id=other, device_id_type=MESH)

    def origin(d, s):
        return (z - s + NZ) % NZ if d == 0 else (z + s) % NZ

    def block(xl_, z_, c_):
        return xl_ * (2 * NZ) + z_ * 2 + c_

    def x_ref_part(xl_, zo, p):
        at = block(xl_, zo, c)
        if p == 0:
            return wbuf.at[at, 0, :, pl.ds(EARLY, share - EARLY), :]
        return wbuf.at[at, 0, :, pl.ds(0, EARLY), :] if p == 3 else wbuf.at[at, p]

    def whole(xl_, z_, c_):
        return wbuf.at[block(xl_, z_, c_)]

    def z_ref(zo, p):
        return x_ref_part(1 - xl, zo, 3) if p == 0 else wbuf.at[block(xl, zo, c), p - 1]

    def remote(ref, send, recv, device):
        return pltpu.make_async_remote_copy(
            src_ref=ref, dst_ref=ref, send_sem=send, recv_sem=recv, device_id=device, device_id_type=MESH
        )

    def z_send(d, s, p):
        return remote(z_ref(origin(d, s - 1), p), zs.at[d, s, p], zr.at[d, s, p], z_next[d])

    def z_recv(d, s, p):
        return remote(z_ref(origin(d, s), p), zs.at[d, s, p], zr.at[d, s, p], z_next[d])

    def x_send(d, s, p):
        return remote(x_ref_part(xl, origin(d, s), p), xs.at[d, s, p], xr.at[d, s, p], cross if p == 2 else x_dev)

    def x_recv(d, s, p):
        return remote(x_ref_part(1 - xl, origin(d, s), p), xs.at[d, s, p], xr.at[d, s, p], cross if p == 2 else x_dev)

    def c_send(d, s, k):
        return remote(whole((xl + k) % 2, origin(d, s), c), cs.at[d, s, k], cr.at[d, s, k], c_dev)

    def c_recv(d, s, k):
        return remote(whole((xl + k) % 2, origin(d, s), 1 - c), cs.at[d, s, k], cr.at[d, s, k], c_dev)

    def weight_rows(first, count):
        return jnp.concatenate(
            [
                wbuf[pl.ds(first, count), j, i].reshape(count * share, HD)
                for i in range(3)
                for j in range(heads)
            ],
            axis=1,
        )

    def multiply(s):
        zc = jnp.where((z + s) % 2 == 1, (z + s) % NZ, (z - s + NZ) % NZ) // 2
        for half in range(2):
            unit = half * (NZ // 2) + zc
            cols = pl.ds(pl.multiple_of(unit * (4 * share), 128), 4 * share)
            acc[...] += jnp.dot(xw[:, cols], weight_rows(unit * 4, 4), preferred_element_type=jnp.float32)

    def move_copy(k, quarter_at, device):
        ref = mbuf.at[quarter_at]
        cols = pl.ds(pl.multiple_of(y * quarter, HD), quarter)
        src = x_ref.at[pl.ds(CAP, MOVE), cols] if k == 0 else ref
        return pltpu.make_async_remote_copy(
            src_ref=src, dst_ref=ref, send_sem=ms.at[k], recv_sem=mr.at[k], device_id=device, device_id_type=MESH
        )

    def move_send(k):
        return move_copy(k, y, cross if k == 0 else (dp, ((y + k) % NY) * 2 + xh))

    def move_recv(k):
        return move_copy(k, (y - k + NY) % NY, cross)

    def swap(k, src, dst, device):
        return pltpu.make_async_remote_copy(
            src_ref=src, dst_ref=dst, send_sem=ps.at[k], recv_sem=pr.at[k], device_id=device, device_id_type=MESH
        )

    def with_sib(k, src, dst):
        return pltpu.make_async_remote_copy(
            src_ref=src, dst_ref=dst, send_sem=bs.at[k], recv_sem=br.at[k], device_id=sib, device_id_type=MESH
        )

    pair, lone = pl.ds(0, 2), pl.ds(2, 1)
    moved, tail = pl.ds(CAP, MOVE), pl.ds(BASE, MOVE)
    grads_swaps = (
        swap(0, gs.at[pair, moved], gm.at[pair], x_dev),
        swap(1, gs.at[lone, moved], gm.at[lone], cross),
    )
    att_swaps = (
        swap(2, attw.at[pair, tail], am.at[pair], x_dev),
        swap(3, attw.at[lone, tail], am.at[lone], cross),
    )
    out_swap = swap(4, outw, om, x_dev)
    weight_sib = with_sib(0, wrem, wbuf.at[b_own, 2])
    grads_sib = with_sib(1, grem, gs.at[2])
    att_sib = with_sib(2, ats.at[2], arem)

    def head(k):
        return pl.ds(pl.multiple_of(k * HD, HD), HD)

    kept = (head(xh), head(xh + 1))
    spare = head(2 - 2 * xh)
    same = xl == 0
    own_rows = pltpu.make_async_copy(x_ref.at[pl.ds(0, CAP)], xw, lsem)

    own_rows.start()
    for i in range(3):
        wrem[i] = w_ref[i, :, spare]
    for j in range(2):
        for i in range(3):
            wbuf[b_own, j, i] = w_ref[i, :, kept[j]]

    @pl.when(same)
    def _():
        wbuf[b_own, 2] = wrem[...]

    grem[...] = g_ref[:, spare]
    for j in range(2):
        gs[j] = g_ref[:, kept[j]]

    @pl.when(same)
    def _():
        gs[2] = grem[...]

    acc[...] = jnp.zeros_like(acc)
    own_ids = column(ids_ref, dp)
    other_ids = column(ids_ref, dev(1 - xl, z, c)[0])
    own_live = own_ids[:, :1] >= 0.0
    taken = [
        jnp.where(own >= 0.0, own, other)
        for own, other in zip(units(own_ids, BASE), units(other_ids, CAP)[::-1], strict=True)
    ]
    work_ids = jnp.concatenate([own_ids[:BASE], *taken], axis=0)
    pl.semaphore_wait(barrier, len(everyone))

    @pl.when(xl == 1)
    def _():
        weight_sib.start()

    for p in (3, 0, 1):
        x_send(0, 0, p).start()
    for p in (1, 2):
        for d in range(2):
            z_send(d, 1, p).start()

    @pl.when(xl == 1)
    def _():
        grads_sib.start()
        weight_sib.wait_recv()

    x_send(0, 0, 2).start()
    for d in range(2):
        z_send(d, 1, 3).start()
    c_send(0, 0, 0).start()
    x_recv(0, 0, 3).wait_recv()
    for d in range(2):
        z_send(d, 1, 0).start()
    move_send(0).start()

    def fill():
        for k in range(1, NY):
            move_recv(k).wait_recv()
        own_rows.wait()
        for at in range(MOVE // UNIT):
            mask = own_live[BASE + at * UNIT : BASE + (at + 1) * UNIT]
            rows = pl.ds(BASE + at * UNIT, UNIT)
            back = pl.ds(MOVE - (at + 1) * UNIT, UNIT)
            for q in range(NY):
                cols = pl.ds(q * quarter, quarter)
                xw[rows, cols] = pick(mask, xw[rows, cols], mbuf[q, back, :])

    order = (1, 2, 3, 0)
    last = {1: 0, 2: 1, 3: 1, 0: 0}
    far = NZ // 2

    def pass_x(d, s):
        for p in range(3):
            x_recv(d, s, p).wait_recv()
        c_send(d, s, 1).start()

    def landed(ds, s):
        for d in ds:
            for k in range(2):
                c_recv(d, s, k).wait_recv()

    def step(s, carry):
        for p in order:
            for d in range(2):
                z_recv(d, s, p).wait_recv()
                if last[p] == d:
                    z_send(d, s + 1, p).start()
                else:
                    @pl.when(s < far - 1)
                    def _():
                        z_send(d, s + 1, p).start()
                if p >= 1:
                    x_send(d, s, p - 1).start()
        for d in range(2):
            c_send(d, s, 0).start()

        @pl.when(s == 1)
        def _():
            pass_x(0, 0)

        @pl.when(s == 2)
        def _():
            landed((0,), 0)
            move_recv(0).wait_recv()
            for k in range(1, NY):
                move_send(k).start()

            @pl.when(xl == 1)
            def _():
                grads_sib.wait_recv()

            for copy in grads_swaps:
                copy.start()

        @pl.when(s > 1)
        def _():
            for d in range(2):
                pass_x(d, s - 1)

        @pl.when(s > 2)
        def _():
            landed((0, 1), s - 2)

        @pl.when(s == FILL)
        def _():
            fill()

        @pl.when(s >= FILL)
        def _():
            multiply(2 * (s - FILL) + 1)

        @pl.when((s >= FILL) & (s < far - 1))
        def _():
            multiply(2 * (s - FILL) + 2)

        return carry

    lax.fori_loop(1, far, step, 0)
    for p in order:
        z_recv(last[p], far, p).wait_recv()
        if p >= 1:
            x_send(0, far, p - 1).start()
    c_send(0, far, 0).start()
    for d in range(2):
        pass_x(d, far - 1)
    landed((0, 1), far - 2)
    multiply(far - 2)
    pass_x(0, far)
    landed((0, 1), far - 1)
    multiply(far - 1)
    landed((0,), far)
    multiply(far)

    qkv[...] = acc[...].astype(jnp.bfloat16)
    row_ids = work_ids.T[:1]
    allowed = (work_ids[:, :1] == row_ids) & (row_ids >= 0.0)
    live = (work_ids[:, :1] >= 0.0).astype(jnp.float32)
    for copy in grads_swaps:
        copy.wait_recv()
    for j in range(heads):
        gw[j, pl.ds(0, BASE)] = gs[j, pl.ds(0, BASE)]
        for at in range(MOVE // UNIT):
            rows = pl.ds(BASE + at * UNIT, UNIT)
            mask = own_live[BASE + at * UNIT : BASE + (at + 1) * UNIT]
            gw[j, rows] = pick(mask, gs[j, rows], gm[j, pl.ds(MOVE - (at + 1) * UNIT, UNIT)])
    for h in range(heads):
        at = [slice(i * width + h * HD, i * width + (h + 1) * HD) for i in range(3)]
        attended, *grads = attend_head(
            qkv[:, at[0]], qkv[:, at[1]], qkv[:, at[2]], gw[h], allowed, live
        )
        attw[h] = attended
        for i in range(3):
            gbuf[:, at[i]] = grads[i]

    for copy in att_swaps:
        copy.start()

    blocks = wbuf.shape[0] // 8

    def dest(i):
        k = i // 2
        dy = jnp.where(k < 2, 2 * k + 1, jnp.where(k == 2, 2, 0))
        return ((y + dy) % NY) * 2 + (xh + 1 - i % 2) % 2

    parts = (pl.ds(BASE, MOVE), pl.ds(0, BASE // 2), pl.ds(BASE // 2, BASE // 2))

    def sums(i, b):
        return pltpu.make_async_remote_copy(
            src_ref=sbuf.at[i, parts[b]], dst_ref=rbuf.at[i, parts[b]], send_sem=ts.at[b, i], recv_sem=tr.at[b, i],
            device_id=(dp, dest(i)), device_id_type=MESH,
        )

    def backward(i, carry):
        rows = weight_rows(dest(i) * blocks, blocks)
        sbuf[i] = lax.dot_general(
            gbuf[...], rows, (((1,), (1,)), ((), ())), preferred_element_type=jnp.float32
        ).astype(jnp.bfloat16)

        @pl.when(i < 7)
        def _():
            sums(i, 0).start()

        return carry

    lax.fori_loop(0, 8, backward, 0)

    for b in (1, 2):

        def rest(i, carry, b=b):
            sums(i, b).start()
            return carry

        lax.fori_loop(0, 7, rest, 0)

    for p in range(4):
        x_send(0, 0, p).wait_send()
    for k in range(2):
        c_send(0, 0, k).wait_send()

    def drain(s, carry):
        for d in range(2):
            for p in range(4):
                z_send(d, s, p).wait_send()
            for p in range(3):
                x_send(d, s, p).wait_send()
            for k in range(2):
                c_send(d, s, k).wait_send()
        return carry

    lax.fori_loop(1, NZ // 2, drain, 0)
    for p in range(4):
        z_send(last[p], far, p).wait_send()
    for p in range(3):
        x_send(0, far, p).wait_send()
    for k in range(2):
        c_send(0, far, k).wait_send()

    for k in range(NY):
        move_send(k).wait_send()
    for copy in grads_swaps:
        copy.wait_send()

    def give(ref, work, received):
        for at in range(MOVE // UNIT):
            for first, rows, index in ((BASE, work, at), (CAP, received, MOVE // UNIT - 1 - at)):
                here = first + at * UNIT
                if rows is not None:
                    mask = own_live[here : here + UNIT]
                    ref[pl.ds(here, UNIT)] = pick(mask, rows[pl.ds(index * UNIT, UNIT)], None)

    for copy in att_swaps:
        copy.wait()
    for j in range(heads):
        ats[j, pl.ds(0, BASE)] = attw[j, pl.ds(0, BASE)]
        give(ats.at[j], attw.at[j, tail], am.at[j])

    @pl.when(xl == 1)
    def _():
        att_sib.start()
        weight_sib.wait_send()
        grads_sib.wait_send()

    for j in range(2):
        att_ref[:, kept[j]] = ats[j]

    @pl.when(same)
    def _():
        att_ref[:, spare] = ats[2]

    def added(b):
        total = sbuf[7, parts[b]].astype(jnp.float32)
        for i in range(7):
            sums(i, b).wait_recv()
            total += rbuf[i, parts[b]].astype(jnp.float32)
        return total.astype(jnp.bfloat16)

    outw[...] = added(0)
    out_swap.start()

    @pl.when(xl == 1)
    def _():
        att_sib.wait()
        att_ref[:, spare] = arem[...]

    give(out_ref, outw, None)
    for b in (1, 2):
        out_ref[parts[b]] = added(b)
    out_swap.wait()
    give(out_ref, None, om)
    for b in range(3):
        for i in range(7):
            sums(i, b).wait_send()


def deliver_kernel(a_ref, b_ref, c_ref, d_ref):
    c_ref[...] = a_ref[...]
    d_ref[...] = b_ref[...]


def deliver(*arrays):
    vmem = pl.BlockSpec(memory_space=pltpu.VMEM)
    return pl.pallas_call(
        deliver_kernel,
        out_shape=tuple(jax.ShapeDtypeStruct(a.shape, a.dtype) for a in arrays),
        in_specs=[vmem] * 2,
        out_specs=(vmem, vmem),
    )(*arrays)


def local(patches, qkv_weight, out_grad, image_starts):
    rows, model = patches.shape
    share = qkv_weight.shape[0]
    columns = qkv_weight.shape[1] * qkv_weight.shape[2]
    n_dp = model // share
    heads = columns // (3 * HD)
    vmem = pl.BlockSpec(memory_space=pltpu.VMEM)
    bf = jnp.bfloat16
    dma = pltpu.SemaphoreType.DMA
    steps = NZ // 2 + 1
    attended, patch_grad = pl.pallas_call(
        kernel,
        out_shape=(
            jax.ShapeDtypeStruct(out_grad.shape, bf),
            jax.ShapeDtypeStruct((rows, model // 8), bf),
        ),
        in_specs=[pl.BlockSpec(memory_space=pl.ANY), vmem, vmem, vmem],
        out_specs=(vmem, vmem),
        scratch_shapes=[
            pltpu.VMEM((n_dp, heads, 3, share, HD), bf),
            pltpu.VMEM((CAP, columns), jnp.float32),
            pltpu.VMEM((CAP, columns), bf),
            pltpu.VMEM((CAP, columns), bf),
            pltpu.VMEM((8, CAP, model // 8), bf),
            pltpu.VMEM((7, CAP, model // 8), bf),
            pltpu.VMEM((CAP, model), bf),
            pltpu.VMEM((NY, MOVE, model // NY), bf),
            pltpu.VMEM((3, share, HD), bf),
            pltpu.VMEM((rows, HD), bf),
            pltpu.VMEM((heads, rows, HD), bf),
            pltpu.VMEM((heads, CAP, HD), bf),
            pltpu.VMEM((heads, MOVE, HD), bf),
            pltpu.VMEM((heads, CAP, HD), bf),
            pltpu.VMEM((heads, MOVE, HD), bf),
            pltpu.VMEM((heads, rows, HD), bf),
            pltpu.VMEM((rows, HD), bf),
            pltpu.VMEM((MOVE, model // 8), bf),
            pltpu.VMEM((MOVE, model // 8), bf),
            dma((2, steps, 4)),
            dma((2, steps, 4)),
            dma((2, steps, 4)),
            dma((2, steps, 4)),
            dma((2, steps, 2)),
            dma((2, steps, 2)),
            dma((3, 8)),
            dma((3, 8)),
            dma((NY,)),
            dma((NY,)),
            dma((5,)),
            dma((5,)),
            dma((3,)),
            dma((3,)),
            dma(()),
        ],
        compiler_params=pltpu.CompilerParams(
            collective_id=0, has_side_effects=True, vmem_limit_bytes=56 * 1024 * 1024
        ),
    )(patches, qkv_weight.transpose(1, 0, 2), out_grad, image_starts)
    return deliver(attended, patch_grad)


def solution(mesh):
    in_specs = (P("dp", None), P("dp", None, "tensor"), P("dp", "tensor"), P())
    out_specs = (P("dp", "tensor"), P("dp", "tensor"))
    return jax.shard_map(local, mesh=mesh, in_specs=in_specs, out_specs=out_specs, check_vma=False)
```
